256 devices in a mesh: az: 32 (over x_lo, z, core), rad: 8 (over y, x_hi).
Axes of the slice: x: 4 (x_hi: 2, x_lo: 2; x = x_hi * 2 + x_lo), y: 4, z: 8, core: 2. Of those that a mesh axis runs over, the one named last changes fastest.
Arguments:
- state: float32 [8, 16, 256, 4096], P(None, None, 'rad', 'az'), may hold values from -6 to 6
- shift_counts: int32 [256], P('rad'), may hold values from 0 to 4095, as said below
- residual_speed: float32 [256], P('rad'), may hold values from -0.5 to 0.5
Outputs:
- evolved: float32 [8, 16, 256, 4096], P(None, None, 'rad', 'az')
The draws below stay inside these ranges and needn't reach their ends.
Inputs may be any that keep to these rules, and one draw needn't show every extreme that they name: `shift_counts`: some row carries by 0 cells and some by 4096 - 1 cells in every draw.
All inputs are finite; a program needn't handle non-finite values.
Results may differ from the reference program's by a relative error of at most 0.00002.
Values sent between devices are 32-bit elements; how exact they have to be, the bound alone decides.
A program may use at most 128 MiB of HBM per device.

```python
import jax
import jax.numpy as jnp
from jax import lax

FIELDS = 8
NZ = 16
STEPS = 2
NR = 256
NAZ = 4096


def draw_shift_counts(key, part):
    values = jax.random.randint(key, (NR,), 0, NAZ, dtype=jnp.int32)
    places = jax.random.permutation(jax.random.fold_in(key, 7), NR)
    values = values.at[places[0]].set(NAZ - 1)
    values = values.at[places[1]].set(0)
    return values


def shard_levels(key, dims, shards, low, high):
    level = 1.0
    for dim, blocks in shards:
        heights = jax.random.uniform(jax.random.fold_in(jax.random.fold_in(key, 6), dim), (blocks,), jnp.float32, low / len(shards), high / len(shards))
        level = level * jnp.repeat(jnp.exp(heights), dims[dim] // blocks).reshape((-1,) + (1,) * (len(dims) - 1 - dim))
    return level


def normal_values(own_key, shape, width, most, pieces=(), kind=jnp.bfloat16):
    gain = shard_levels(own_key, shape, pieces, -0.22, 0.18) if pieces else 1.0
    result = jax.random.normal(own_key, shape, jnp.float32) * width * gain
    return jnp.minimum(jnp.maximum(result, -most), most).astype(kind)


def setup_inputs(seed: int = 0) -> dict:
    splits = jax.random.split(jax.random.key(seed), 4)
    state = normal_values(splits[0], (FIELDS, NZ, NR, NAZ), 1.0, 6.0, ((2, 8), (3, 32)), jnp.float32)
    shift_counts = draw_shift_counts(jax.random.fold_in(splits[3], 71), 0)
    residual_speed = jnp.clip(jax.random.uniform(splits[2], (NR,), jnp.float32, -0.5, 0.5) * shard_levels(splits[2], (NR,), ((0, 8),), -0.4, 0.0), -0.5, 0.5)
    return dict(state=state, shift_counts=shift_counts, residual_speed=residual_speed)


time_step = 0.2
viscosity = 0.1
shear_rate = 1.5


def shift_field(field, counts):
    columns = jnp.arange(NAZ, dtype=jnp.int32)
    source = (columns[None, :] - counts[:, None].astype(jnp.int32)) % NAZ
    return jnp.take_along_axis(field, jnp.broadcast_to(source[None], field.shape), axis=2)


def transport(fields, lower, upper, speed):
    weight = speed[None, None, :, None]
    forward = jnp.maximum(weight, 0.0)
    backward = jnp.minimum(weight, 0.0)
    return fields - forward * (fields - lower) - backward * (upper - fields)


def update(fields, padded, omega):
    north = padded[:, :, 2:]
    south = padded[:, :, :-2]
    radial_diff = (north - south) * 0.5
    radial_lap = north - 2.0 * fields + south
    upward = jnp.roll(fields, -1, 1)
    downward = jnp.roll(fields, 1, 1)
    vertical_diff = (upward - downward) * 0.5
    vertical_lap = upward - 2.0 * fields + downward
    spin = omega[None, :, None]
    rates = [
        -(radial_diff[1] + vertical_diff[3]),
        -radial_diff[0] + 2.0 * spin * fields[2] + vertical_diff[4],
        -(2.0 - shear_rate) * spin * fields[1] + vertical_diff[5],
        -vertical_diff[0],
        vertical_diff[1],
        vertical_diff[2] - shear_rate * spin * fields[4],
        -radial_diff[1],
        -(radial_diff[1] + vertical_diff[3]),
    ]
    return fields + viscosity * (radial_lap + vertical_lap) + time_step * jnp.stack(rates)


def reference(state, shift_counts, residual_speed):
    radius = jnp.arange(NR).astype(jnp.float32)
    omega = (1.0 + radius / NR) ** -1.5
    fields = state
    for step_index in range(STEPS):
        fields = lax.map(lambda single: shift_field(single, shift_counts), fields)
        fields = transport(fields, jnp.roll(fields, 1, 3), jnp.roll(fields, -1, 3), residual_speed)
        padded = jnp.pad(fields, ((0, 0), (0, 0), (1, 1), (0, 0)))
        fields = update(fields, padded, omega)
    return fields
```

```python
import jax
import jax.numpy as jnp
from jax import lax
from jax.experimental import pallas as pl
from jax.experimental.pallas import tpu as pltpu
from jax.sharding import PartitionSpec as P

FIELDS, NZ, ROWS, LANES = 8, 16, 32, 128
AZ, RAD = 32, 8
Z_CHIPS = 8
PART = 4
ORDER = (0, 3, 1, 2)

time_step = 0.2
viscosity = 0.1
shear_rate = 1.5

MESH = pl.DeviceIdType.MESH


def place(index, rad):
    core = lax.rem(index, 2)
    z = lax.rem(index // 2, Z_CHIPS)
    x = index // (2 * Z_CHIPS)
    block = z + lax.rem(rad, 2) * (Z_CHIPS - 1 - 2 * z)
    quarter = 2 * x + lax.rem(core + x, 2)
    return block, quarter


def owner(block, quarter, rad):
    z = block + lax.rem(rad, 2) * (Z_CHIPS - 1 - 2 * block)
    x = quarter // 2
    core = lax.rem(lax.rem(quarter, 2) + x, 2)
    return (x * Z_CHIPS + z) * 2 + core


def field_vector(values):
    row = lax.broadcasted_iota(jnp.int32, (FIELDS, LANES), 0)
    first = values[0]
    result = jnp.full((FIELDS, LANES), first, jnp.asarray(first).dtype)
    for index in range(1, FIELDS):
        result = jnp.where(row == index, values[index], result)
    return result


def picked(value, source):
    count = value.shape[0]
    flat = value.reshape(count * FIELDS, LANES)
    parts = [
        jnp.take_along_axis(flat[i * FIELDS : (i + 1) * FIELDS], source, axis=0)
        for i in range(count)
    ]
    return jnp.stack(parts)


def evolve(v, north, south, up, down, spin):
    from_radial = field_vector([1, 0, 2, 3, 4, 5, 1, 1])
    from_vertical = field_vector([3, 4, 5, 0, 1, 2, 6, 3])
    from_spin = field_vector([0, 2, 1, 3, 4, 4, 6, 7])
    half = 0.5 * time_step
    radial_factor = field_vector([-half, -half, 0.0, 0.0, 0.0, 0.0, -half, -half])
    vertical_factor = field_vector([-half, half, half, -half, half, half, 0.0, -half])
    spin_factor = field_vector(
        [
            0.0,
            2.0 * time_step,
            -(2.0 - shear_rate) * time_step,
            0.0,
            0.0,
            -shear_rate * time_step,
            0.0,
            0.0,
        ]
    )
    laplacian = (north + south) + (up + down) - 4.0 * v
    rates = (
        radial_factor * picked(north - south, from_radial)
        + vertical_factor * picked(up - down, from_vertical)
        + (spin_factor * spin) * picked(v, from_spin)
    )
    return v + viscosity * laplacian + rates


def transport(source, target, speed):
    forward = jnp.maximum(speed, 0.0)
    backward = jnp.minimum(speed, 0.0)

    def body(k, carry):
        shape = (PART * FIELDS, LANES)
        lane = lax.broadcasted_iota(jnp.int32, shape, 1)
        here = source[k].reshape(shape)
        before = source[lax.rem(k + AZ - 1, AZ)].reshape(shape)
        after = source[lax.rem(k + 1, AZ)].reshape(shape)
        lower = pltpu.roll(jnp.where(lane == LANES - 1, before, here), 1, 1)
        upper = pltpu.roll(jnp.where(lane == 0, after, here), LANES - 1, 1)
        moved = here - forward * (here - lower) - backward * (upper - here)
        target[k] = moved.reshape(PART, FIELDS, LANES)
        return carry

    lax.fori_loop(0, AZ, body, 0, unroll=2)


def rotate(source, target, count):
    hops = count // LANES
    lanes = lax.rem(count, LANES)

    def body(k, carry):
        shape = (PART * FIELDS, LANES)
        lane = lax.broadcasted_iota(jnp.int32, shape, 1)
        here = source[lax.rem(k - hops + AZ, AZ)].reshape(shape)
        before = source[lax.rem(k - hops + 2 * AZ - 1, AZ)].reshape(shape)
        joined = jnp.where(lane >= LANES - lanes, before, here)
        target[k] = pltpu.roll(joined, lanes, 1).reshape(PART, FIELDS, LANES)
        return carry

    lax.fori_loop(0, AZ, body, 0, unroll=2)


def kernel(
    state, counts, speeds, spins, out,
    packed, wide, moved, evolved, *scratch,
):
    received = scratch[0:4]
    carried = scratch[4:8]
    ready = scratch[8:12]
    cell_below = scratch[12:16]
    cell_above = scratch[16:20]
    row_south, row_north = scratch[20:22]
    (in_send, in_recv, out_send, out_recv, own, up_send, up_recv, down_send, down_recv,
     row_send, row_recv, edge_send, edge_recv) = scratch[22:]

    me = lax.axis_index("az")
    rad = lax.axis_index("rad")
    rad_next = lax.rem(rad + 1, RAD)
    rad_last = lax.rem(rad + RAD - 1, RAD)
    block, quarter = place(me, rad)

    barrier = pltpu.get_barrier_semaphore()

    def greet(k, carry):
        pl.semaphore_signal(
            barrier, inc=1, device_id={"az": lax.rem(me + k, AZ)}, device_id_type=MESH
        )
        return carry

    lax.fori_loop(1, AZ, greet, 0)
    for other in (rad_next, rad_last):
        pl.semaphore_signal(barrier, inc=1, device_id={"rad": other}, device_id_type=MESH)

    def pack(row, carry):
        for cell in range(NZ):
            packed[row, cell] = state[pl.ds(cell * ROWS + row, FIELDS, stride=NZ * ROWS), :]
        return carry

    lax.fori_loop(0, ROWS, pack, 0)
    pl.semaphore_wait(barrier, AZ + 1)

    def send_in(c):
        own_copy = pltpu.make_async_copy(
            packed.at[PART * block + c, pl.ds(PART * quarter, PART)], received[c].at[me], own.at[c]
        )
        own_copy.start()

        def body(k, carry):
            to = lax.rem(me + k, AZ)
            to_block, to_quarter = place(to, rad)
            pltpu.make_async_remote_copy(
                src_ref=packed.at[PART * to_block + c, pl.ds(PART * to_quarter, PART)],
                dst_ref=received[c].at[me],
                send_sem=in_send.at[c],
                recv_sem=in_recv.at[c],
                device_id={"az": to},
                device_id_type=MESH,
            ).start()
            return carry

        lax.fori_loop(1, AZ, body, 0)
        return own_copy

    def send_out(c):
        own_copy = pltpu.make_async_copy(
            ready[c].at[me], wide.at[1 + PART * block + c, pl.ds(PART * quarter, PART)],
            own.at[PART + c],
        )
        own_copy.start()

        def body(k, carry):
            to = lax.rem(me + k, AZ)
            pltpu.make_async_remote_copy(
                src_ref=ready[c].at[to],
                dst_ref=wide.at[1 + PART * block + c, pl.ds(PART * quarter, PART)],
                send_sem=out_send.at[c],
                recv_sem=out_recv.at[c],
                device_id={"az": to},
                device_id_type=MESH,
            ).start()
            return carry

        lax.fori_loop(1, AZ, body, 0)
        return own_copy

    def whole(buffer, send_sem, recv_sem):
        part = buffer.at[pl.ds(0, AZ - 1)]
        return pltpu.make_async_remote_copy(
            src_ref=part, dst_ref=part, send_sem=send_sem, recv_sem=recv_sem,
            device_id={"az": lax.rem(me + 1, AZ)}, device_id_type=MESH,
        )

    def cells(c):
        to_down = owner(block, lax.rem(quarter + 3, 4), rad)
        to_up = owner(block, lax.rem(quarter + 1, 4), rad)
        down = pltpu.make_async_remote_copy(
            src_ref=carried[c].at[:, 0], dst_ref=cell_above[c],
            send_sem=down_send.at[c], recv_sem=down_recv.at[c],
            device_id={"az": to_down}, device_id_type=MESH,
        )
        up = pltpu.make_async_remote_copy(
            src_ref=carried[c].at[:, PART - 1], dst_ref=cell_below[c],
            send_sem=up_send.at[c], recv_sem=up_recv.at[c],
            device_id={"az": to_up}, device_id_type=MESH,
        )
        down.start()
        up.start()
        return down, up

    def row_copy(which, source, target, step):
        other = block + step
        to_rad = lax.rem(rad + (other + Z_CHIPS) // Z_CHIPS - 1 + RAD, RAD)
        to_block = lax.rem(other + Z_CHIPS, Z_CHIPS)
        copy = pltpu.make_async_remote_copy(
            src_ref=source, dst_ref=target,
            send_sem=row_send.at[which], recv_sem=row_recv.at[which],
            device_id={"az": owner(to_block, quarter, to_rad), "rad": to_rad},
            device_id_type=MESH,
        )
        copy.start()
        return copy

    def first_step(c):
        row = PART * block + c
        transport(received[c], moved, speeds[row])
        rotate(moved, carried[c], counts[row])

    has_south = jnp.logical_or(rad > 0, block > 0)
    has_north = jnp.logical_or(rad < RAD - 1, block < Z_CHIPS - 1)

    def second_step(c):
        row = PART * block + c
        spin = spins[row]

        def body(k, carry):
            v = carried[c][k]
            if c > 0:
                south = carried[c - 1][k]
            else:
                south = row_south[k]
                south = jnp.where(has_south, south, jnp.zeros_like(south))
            if c < PART - 1:
                north = carried[c + 1][k]
            else:
                north = row_north[k]
                north = jnp.where(has_north, north, jnp.zeros_like(north))
            up = jnp.concatenate([v[1:], cell_above[c][k][None]], axis=0)
            down = jnp.concatenate([cell_below[c][k][None], v[:-1]], axis=0)
            evolved[k] = evolve(v, north, south, up, down, spin)
            return carry

        lax.fori_loop(0, AZ, body, 0)
        transport(evolved, moved, speeds[row])
        rotate(moved, ready[c], counts[row])

    ins, outs, halos = {}, {}, {}

    def wait_in(c):
        ins[c].wait()
        whole(received[c], in_send.at[c], in_recv.at[c]).wait_recv()

    def wait_cells(c):
        for copy in halos[c]:
            copy.wait_recv()

    def wait_out(c):
        outs[c].wait()
        whole(ready[c], out_send.at[c], out_recv.at[c]).wait_recv()

    ins[0] = send_in(0)
    ins[3] = send_in(3)

    wait_in(0)
    ins[1] = send_in(1)
    first_step(0)
    to_last = row_copy(0, carried[0], row_north, -1)
    halos[0] = cells(0)

    wait_in(3)
    ins[2] = send_in(2)
    first_step(3)
    to_next = row_copy(1, carried[3], row_south, 1)
    halos[3] = cells(3)

    wait_in(1)
    first_step(1)
    halos[1] = cells(1)

    to_next.wait_recv()
    wait_cells(0)
    second_step(0)
    outs[0] = send_out(0)

    wait_in(2)
    first_step(2)
    halos[2] = cells(2)

    to_last.wait_recv()
    wait_cells(3)
    second_step(3)
    outs[3] = send_out(3)
    for c in (1, 2):
        wait_cells(c)
        second_step(c)
        outs[c] = send_out(c)

    def edge(which, source, target, to):
        copy = pltpu.make_async_remote_copy(
            src_ref=wide.at[source], dst_ref=wide.at[target],
            send_sem=edge_send.at[which], recv_sem=edge_recv.at[which],
            device_id={"rad": to}, device_id_type=MESH,
        )
        copy.start()
        return copy

    wait_out(0)
    edge_last = edge(0, 1, ROWS + 1, rad_last)
    wait_out(3)
    edge_next = edge(1, ROWS, 0, rad_next)
    wait_out(1)
    wait_out(2)
    edge_last.wait()
    edge_next.wait()

    @pl.when(rad == 0)
    def _():
        wide[0] = jnp.zeros((NZ, FIELDS, LANES), jnp.float32)

    @pl.when(rad == RAD - 1)
    def _():
        wide[ROWS + 1] = jnp.zeros((NZ, FIELDS, LANES), jnp.float32)

    def last(row, carry):
        spin = spins[row]
        for cell in range(NZ):
            pick = lambda r, c: wide[r, c][None]
            result = evolve(
                pick(row + 1, cell), pick(row + 2, cell), pick(row, cell),
                pick(row + 1, (cell + 1) % NZ), pick(row + 1, (cell + NZ - 1) % NZ), spin,
            )
            out[pl.ds(cell * ROWS + row, FIELDS, stride=NZ * ROWS), :] = result[0]
        return carry

    lax.fori_loop(0, ROWS, last, 0)

    for c in ORDER:
        whole(received[c], in_send.at[c], in_recv.at[c]).wait_send()
        whole(ready[c], out_send.at[c], out_recv.at[c]).wait_send()
        for copy in halos[c]:
            copy.wait_send()
    to_last.wait_send()
    to_next.wait_send()


def shards(state, shift_counts, residual_speed):
    radius = (lax.axis_index("rad") * ROWS + jnp.arange(ROWS, dtype=jnp.int32)).astype(jnp.float32)
    omega = (1.0 + radius / (ROWS * RAD)) ** (-1.5)
    circle = (AZ, PART, FIELDS, LANES)
    vmem = pl.BlockSpec(memory_space=pltpu.VMEM)
    smem = pl.BlockSpec(memory_space=pltpu.SMEM)
    f32 = jnp.float32
    dma = pltpu.SemaphoreType.DMA
    result = pl.pallas_call(
        kernel,
        out_shape=jax.ShapeDtypeStruct((FIELDS * NZ * ROWS, LANES), f32),
        in_specs=[vmem, smem, smem, smem],
        out_specs=vmem,
        scratch_shapes=[
            pltpu.VMEM((ROWS, NZ, FIELDS, LANES), f32),
            pltpu.VMEM((ROWS + 2, NZ, FIELDS, LANES), f32),
            pltpu.VMEM(circle, f32),
            pltpu.VMEM(circle, f32),
        ]
        + [pltpu.VMEM(circle, f32)] * 12
        + [pltpu.VMEM((AZ, FIELDS, LANES), f32)] * 8
        + [pltpu.VMEM(circle, f32)] * 2
        + [dma((4,)), dma((4,)), dma((4,)), dma((4,)), dma((8,))]
        + [dma((4,)), dma((4,)), dma((4,)), dma((4,))]
        + [dma((2,)), dma((2,)), dma((2,)), dma((2,))],
        compiler_params=pltpu.CompilerParams(
            collective_id=0, has_side_effects=True, vmem_limit_bytes=48 << 20
        ),
    )(state.reshape(FIELDS * NZ * ROWS, LANES), shift_counts, residual_speed, omega)
    return result.reshape(FIELDS, NZ, ROWS, LANES)


def solution(mesh):
    placed = (P(None, None, "rad", "az"), P("rad"), P("rad"))
    return jax.shard_map(
        shards, mesh=mesh, in_specs=placed, out_specs=P(None, None, "rad", "az"), check_vma=False
    )
```

```python
import jax
import jax.numpy as jnp
from jax import lax
from jax.experimental import pallas as pl
from jax.experimental.pallas import tpu as pltpu
from jax.sharding import PartitionSpec as P

FIELDS, NZ, ROWS, LANES = 8, 16, 32, 128
AZ, RAD = 32, 8
Z_CHIPS = 8
PART = 4
ORDER = (0, 3, 1, 2)

time_step = 0.2
viscosity = 0.1
shear_rate = 1.5

MESH = pl.DeviceIdType.MESH


def place(index, rad):
    core = lax.rem(index, 2)
    z = lax.rem(index // 2, Z_CHIPS)
    x = index // (2 * Z_CHIPS)
    block = z + lax.rem(rad, 2) * (Z_CHIPS - 1 - 2 * z)
    quarter = 2 * x + lax.rem(core + x, 2)
    return block, quarter


def owner(block, quarter, rad):
    z = block + lax.rem(rad, 2) * (Z_CHIPS - 1 - 2 * block)
    x = quarter // 2
    core = lax.rem(lax.rem(quarter, 2) + x, 2)
    return (x * Z_CHIPS + z) * 2 + core


def field_vector(values):
    row = lax.broadcasted_iota(jnp.int32, (FIELDS, LANES), 0)
    first = values[0]
    result = jnp.full((FIELDS, LANES), first, jnp.asarray(first).dtype)
    for index in range(1, FIELDS):
        result = jnp.where(row == index, values[index], result)
    return result


def picked(value, source):
    count = value.shape[0]
    flat = value.reshape(count * FIELDS, LANES)
    parts = [
        jnp.take_along_axis(flat[i * FIELDS : (i + 1) * FIELDS], source, axis=0)
        for i in range(count)
    ]
    return jnp.stack(parts)


def field_tables():
    half = 0.5 * time_step
    return (
        field_vector([1, 0, 2, 3, 4, 5, 1, 1]),
        field_vector([3, 4, 5, 0, 1, 2, 6, 3]),
        field_vector([0, 2, 1, 3, 4, 4, 6, 7]),
        field_vector([-half, -half, 0.0, 0.0, 0.0, 0.0, -half, -half]),
        field_vector([-half, half, half, -half, half, half, 0.0, -half]),
        field_vector(
            [
                0.0,
                2.0 * time_step,
                -(2.0 - shear_rate) * time_step,
                0.0,
                0.0,
                -shear_rate * time_step,
                0.0,
                0.0,
            ]
        ),
    )


def spin_of(row, rad, spin_factor):
    radius = jnp.full((FIELDS, LANES), rad * ROWS + row, jnp.int32).astype(jnp.float32)
    distance = 1.0 + radius / (ROWS * RAD)
    return spin_factor / (distance * jnp.sqrt(distance))


def evolve(v, north, south, up, down, tables, spin):
    from_radial, from_vertical, from_spin, radial_factor, vertical_factor, _ = tables
    laplacian = (north + south) + (up + down) - 4.0 * v
    rates = (
        radial_factor * picked(north - south, from_radial)
        + vertical_factor * picked(up - down, from_vertical)
        + spin * picked(v, from_spin)
    )
    return v + viscosity * laplacian + rates


def carry(source, target, speed, count):
    shape = (PART * FIELDS, LANES)
    forward = jnp.maximum(speed, 0.0)
    backward = jnp.minimum(speed, 0.0)
    hops = count // LANES
    lanes = lax.rem(count, LANES)
    lane = lax.broadcasted_iota(jnp.int32, shape, 1)
    own_mask = lane >= LANES - lanes
    low_mask = lane >= LANES - 1 - lanes
    high_mask = lane >= LANES + 1 - lanes
    next_mask = lane + lanes == 0

    def body(k, nothing):
        here = source[lax.rem(k - hops + AZ, AZ)].reshape(shape)
        before = source[lax.rem(k - hops + 2 * AZ - 1, AZ)].reshape(shape)
        after = source[lax.rem(k - hops + AZ + 1, AZ)].reshape(shape)
        cells = jnp.where(own_mask, before, here)
        lower = pltpu.roll(jnp.where(low_mask, before, here), 1, 1)
        upper = jnp.where(next_mask, after, jnp.where(high_mask, before, here))
        upper = pltpu.roll(upper, LANES - 1, 1)
        moved = cells - forward * (cells - lower) - backward * (upper - cells)
        target[k] = pltpu.roll(moved, lanes, 1).reshape(PART, FIELDS, LANES)
        return nothing

    lax.fori_loop(0, AZ, body, 0, unroll=8)


def kernel(
    state_hbm, counts_hbm, speeds_hbm, out,
    state, counts, speeds, packed, wide, evolved, *scratch,
):
    received = scratch[0:4]
    carried = scratch[4:8]
    ready = scratch[8:12]
    cell_below = scratch[12:16]
    cell_above = scratch[16:20]
    row_south, row_north = scratch[20:22]
    (in_send, in_recv, out_send, out_recv, own, up_send, up_recv, down_send, down_recv,
     row_send, row_recv, edge_send, edge_recv, load) = scratch[22:]

    loads = [
        pltpu.make_async_copy(source, target, load.at[i])
        for i, (source, target) in enumerate(
            [(state_hbm, state), (counts_hbm, counts), (speeds_hbm, speeds)]
        )
    ]

    me = lax.axis_index("az")
    rad = lax.axis_index("rad")
    rad_next = lax.rem(rad + 1, RAD)
    rad_last = lax.rem(rad + RAD - 1, RAD)
    block, quarter = place(me, rad)

    barrier = pltpu.get_barrier_semaphore()

    def greet(k, carry):
        pl.semaphore_signal(
            barrier, inc=1, device_id={"az": lax.rem(me + k, AZ)}, device_id_type=MESH
        )
        return carry

    lax.fori_loop(1, AZ, greet, 0)
    for other in (rad_next, rad_last):
        pl.semaphore_signal(barrier, inc=1, device_id={"rad": other}, device_id_type=MESH)

    for copy in loads:
        copy.start()
    tables = field_tables()

    def pack(c):
        def body(i, carry):
            row = PART * i + c
            for cell in range(NZ):
                packed[row, cell] = state[pl.ds(cell * ROWS + row, FIELDS, stride=NZ * ROWS), :]
            return carry

        lax.fori_loop(0, ROWS // PART, body, 0)

    def partner(k):
        return lax.rem(me + AZ + (k + 1) // 2 * (2 * lax.rem(k, 2) - 1), AZ)

    def send_in(c):
        own_copy = pltpu.make_async_copy(
            packed.at[PART * block + c, pl.ds(PART * quarter, PART)], received[c].at[me], own.at[c]
        )
        own_copy.start()

        def body(k, carry):
            to = partner(k)
            to_block, to_quarter = place(to, rad)
            pltpu.make_async_remote_copy(
                src_ref=packed.at[PART * to_block + c, pl.ds(PART * to_quarter, PART)],
                dst_ref=received[c].at[me],
                send_sem=in_send.at[c],
                recv_sem=in_recv.at[c],
                device_id={"az": to},
                device_id_type=MESH,
            ).start()
            return carry

        lax.fori_loop(1, AZ, body, 0)
        return own_copy

    def send_out(c):
        own_copy = pltpu.make_async_copy(
            ready[c].at[me], wide.at[1 + PART * block + c, pl.ds(PART * quarter, PART)],
            own.at[PART + c],
        )
        own_copy.start()

        def body(k, carry):
            to = partner(k)
            pltpu.make_async_remote_copy(
                src_ref=ready[c].at[to],
                dst_ref=wide.at[1 + PART * block + c, pl.ds(PART * quarter, PART)],
                send_sem=out_send.at[c],
                recv_sem=out_recv.at[c],
                device_id={"az": to},
                device_id_type=MESH,
            ).start()
            return carry

        lax.fori_loop(1, AZ, body, 0)
        return own_copy

    def whole(buffer, send_sem, recv_sem):
        part = buffer.at[pl.ds(0, AZ - 1)]
        return pltpu.make_async_remote_copy(
            src_ref=part, dst_ref=part, send_sem=send_sem, recv_sem=recv_sem,
            device_id={"az": lax.rem(me + 1, AZ)}, device_id_type=MESH,
        )

    def cells(c):
        to_down = owner(block, lax.rem(quarter + 3, 4), rad)
        to_up = owner(block, lax.rem(quarter + 1, 4), rad)
        down = pltpu.make_async_remote_copy(
            src_ref=carried[c].at[:, 0], dst_ref=cell_above[c],
            send_sem=down_send.at[c], recv_sem=down_recv.at[c],
            device_id={"az": to_down}, device_id_type=MESH,
        )
        up = pltpu.make_async_remote_copy(
            src_ref=carried[c].at[:, PART - 1], dst_ref=cell_below[c],
            send_sem=up_send.at[c], recv_sem=up_recv.at[c],
            device_id={"az": to_up}, device_id_type=MESH,
        )
        down.start()
        up.start()
        return down, up

    def row_copy(which, source, target, step):
        other = block + step
        to_rad = lax.rem(rad + (other + Z_CHIPS) // Z_CHIPS - 1 + RAD, RAD)
        to_block = lax.rem(other + Z_CHIPS, Z_CHIPS)
        copy = pltpu.make_async_remote_copy(
            src_ref=source, dst_ref=target,
            send_sem=row_send.at[which], recv_sem=row_recv.at[which],
            device_id={"az": owner(to_block, quarter, to_rad), "rad": to_rad},
            device_id_type=MESH,
        )
        copy.start()
        return copy

    def first_step(c):
        row = PART * block + c
        carry(received[c], carried[c], speeds[row], counts[row])

    has_south = jnp.logical_or(rad > 0, block > 0)
    has_north = jnp.logical_or(rad < RAD - 1, block < Z_CHIPS - 1)

    def second_step(c):
        row = PART * block + c
        spin = spin_of(row, rad, tables[-1])

        def body(k, nothing):
            v = carried[c][k]
            if c > 0:
                south = carried[c - 1][k]
            else:
                south = row_south[k]
                south = jnp.where(has_south, south, jnp.zeros_like(south))
            if c < PART - 1:
                north = carried[c + 1][k]
            else:
                north = row_north[k]
                north = jnp.where(has_north, north, jnp.zeros_like(north))
            up = jnp.concatenate([v[1:], cell_above[c][k][None]], axis=0)
            down = jnp.concatenate([cell_below[c][k][None], v[:-1]], axis=0)
            evolved[k] = evolve(v, north, south, up, down, tables, spin)
            return nothing

        lax.fori_loop(0, AZ, body, 0, unroll=4)
        carry(evolved, ready[c], speeds[row], counts[row])

    ins, outs, halos = {}, {}, {}

    def wait_in(c):
        ins[c].wait()
        whole(received[c], in_send.at[c], in_recv.at[c]).wait_recv()

    def wait_cells(c):
        for copy in halos[c]:
            copy.wait_recv()

    def wait_out(c):
        outs[c].wait()
        whole(ready[c], out_send.at[c], out_recv.at[c]).wait_recv()

    loads[0].wait()
    pack(0)
    pl.semaphore_wait(barrier, AZ + 1)
    ins[0] = send_in(0)
    pack(3)
    ins[3] = send_in(3)
    pack(1)
    pack(2)
    loads[1].wait()
    loads[2].wait()

    wait_in(0)
    ins[1] = send_in(1)
    first_step(0)
    to_last = row_copy(0, carried[0], row_north, -1)
    halos[0] = cells(0)

    wait_in(3)
    ins[2] = send_in(2)
    first_step(3)
    to_next = row_copy(1, carried[3], row_south, 1)
    halos[3] = cells(3)

    wait_in(1)
    first_step(1)
    halos[1] = cells(1)

    to_next.wait_recv()
    wait_cells(0)
    second_step(0)
    outs[0] = send_out(0)

    wait_in(2)
    first_step(2)
    halos[2] = cells(2)

    to_last.wait_recv()
    wait_cells(3)
    second_step(3)
    outs[3] = send_out(3)
    for c in (1, 2):
        wait_cells(c)
        second_step(c)
        outs[c] = send_out(c)

    def edge(which, source, target, to):
        copy = pltpu.make_async_remote_copy(
            src_ref=wide.at[source], dst_ref=wide.at[target],
            send_sem=edge_send.at[which], recv_sem=edge_recv.at[which],
            device_id={"rad": to}, device_id_type=MESH,
        )
        copy.start()
        return copy

    wait_out(0)
    edge_last = edge(0, 1, ROWS + 1, rad_last)
    wait_out(3)
    edge_next = edge(1, ROWS, 0, rad_next)
    edge_last.wait()
    edge_next.wait()

    @pl.when(rad == 0)
    def _():
        wide[0] = jnp.zeros((NZ, FIELDS, LANES), jnp.float32)

    @pl.when(rad == RAD - 1)
    def _():
        wide[ROWS + 1] = jnp.zeros((NZ, FIELDS, LANES), jnp.float32)

    def last(row):
        spin = spin_of(row, rad, tables[-1])
        for cell in range(NZ):
            pick = lambda r, c: wide[r, c][None]
            result = evolve(
                pick(row + 1, cell), pick(row + 2, cell), pick(row, cell),
                pick(row + 1, (cell + 1) % NZ), pick(row + 1, (cell + NZ - 1) % NZ), tables, spin,
            )
            out[pl.ds(cell * ROWS + row, FIELDS, stride=NZ * ROWS), :] = result[0]

    def last_first(i, nothing):
        last(PART * i)
        return nothing

    def last_others(i, nothing):
        for c in range(1, PART):
            last(PART * i + c)
        return nothing

    wait_out(1)
    lax.fori_loop(0, ROWS // PART, last_first, 0)
    wait_out(2)
    lax.fori_loop(0, ROWS // PART, last_others, 0)

    for c in ORDER:
        whole(received[c], in_send.at[c], in_recv.at[c]).wait_send()
        whole(ready[c], out_send.at[c], out_recv.at[c]).wait_send()
        for copy in halos[c]:
            copy.wait_send()
    to_last.wait_send()
    to_next.wait_send()


def shards(state, shift_counts, residual_speed):
    circle = (AZ, PART, FIELDS, LANES)
    vmem = pl.BlockSpec(memory_space=pltpu.VMEM)
    hbm = pl.BlockSpec(memory_space=pltpu.HBM)
    f32 = jnp.float32
    dma = pltpu.SemaphoreType.DMA
    result = pl.pallas_call(
        kernel,
        out_shape=jax.ShapeDtypeStruct((FIELDS * NZ * ROWS, LANES), f32),
        in_specs=[hbm, hbm, hbm],
        out_specs=vmem,
        scratch_shapes=[
            pltpu.VMEM((FIELDS * NZ * ROWS, LANES), f32),
            pltpu.SMEM((ROWS,), jnp.int32),
            pltpu.SMEM((ROWS,), f32),
            pltpu.VMEM((ROWS, NZ, FIELDS, LANES), f32),
            pltpu.VMEM((ROWS + 2, NZ, FIELDS, LANES), f32),
            pltpu.VMEM(circle, f32),
        ]
        + [pltpu.VMEM(circle, f32)] * 12
        + [pltpu.VMEM((AZ, FIELDS, LANES), f32)] * 8
        + [pltpu.VMEM(circle, f32)] * 2
        + [dma((4,)), dma((4,)), dma((4,)), dma((4,)), dma((8,))]
        + [dma((4,)), dma((4,)), dma((4,)), dma((4,))]
        + [dma((2,)), dma((2,)), dma((2,)), dma((2,)), dma((3,))],
        compiler_params=pltpu.CompilerParams(
            collective_id=0, has_side_effects=True, vmem_limit_bytes=48 << 20
        ),
    )(state.reshape(FIELDS * NZ * ROWS, LANES), shift_counts, residual_speed)
    return result.reshape(FIELDS, NZ, ROWS, LANES)


def solution(mesh):
    placed = (P(None, None, "rad", "az"), P("rad"), P("rad"))
    return jax.shard_map(
        shards, mesh=mesh, in_specs=placed, out_specs=P(None, None, "rad", "az"), check_vma=False
    )
```

```python
import jax
import jax.numpy as jnp
from jax import lax
from jax.experimental import pallas as pl
from jax.experimental.pallas import tpu as pltpu
from jax.sharding import PartitionSpec as P

FIELDS, NZ, ROWS, LANES = 8, 16, 32, 128
AZ, RAD = 32, 8
Z_CHIPS = 8
PART = 4
ORDER = (0, 3, 1, 2)
TILES = AZ * PART
BORDER = 7 * TILES
LAST = 2
LAST_PARTS = ((0, 1), (2, 3))

time_step = 0.2
viscosity = 0.1
shear_rate = 1.5

MESH = pl.DeviceIdType.MESH


def place(index, rad):
    core = lax.rem(index, 2)
    z = lax.rem(index // 2, Z_CHIPS)
    x = index // (2 * Z_CHIPS)
    block = z + lax.rem(rad, 2) * (Z_CHIPS - 1 - 2 * z)
    quarter = 2 * x + lax.rem(core + x, 2)
    return block, quarter


def owner(block, quarter, rad):
    z = block + lax.rem(rad, 2) * (Z_CHIPS - 1 - 2 * block)
    x = quarter // 2
    core = lax.rem(lax.rem(quarter, 2) + x, 2)
    return (x * Z_CHIPS + z) * 2 + core


def field_vector(values):
    row = lax.broadcasted_iota(jnp.int32, (FIELDS, LANES), 0)
    first = values[0]
    result = jnp.full((FIELDS, LANES), first, jnp.asarray(first).dtype)
    for index in range(1, FIELDS):
        result = jnp.where(row == index, values[index], result)
    return result


def picked(value, source):
    count = value.shape[0]
    flat = value.reshape(count * FIELDS, LANES)
    parts = [
        jnp.take_along_axis(flat[i * FIELDS : (i + 1) * FIELDS], source, axis=0)
        for i in range(count)
    ]
    return jnp.stack(parts)


def field_tables():
    half = 0.5 * time_step
    return (
        field_vector([1, 0, 2, 3, 4, 5, 1, 1]),
        field_vector([3, 4, 5, 0, 1, 2, 6, 3]),
        field_vector([0, 2, 1, 3, 4, 4, 6, 7]),
        field_vector([-half, -half, 0.0, 0.0, 0.0, 0.0, -half, -half]),
        field_vector([-half, half, half, -half, half, half, 0.0, -half]),
        field_vector(
            [
                0.0,
                2.0 * time_step,
                -(2.0 - shear_rate) * time_step,
                0.0,
                0.0,
                -shear_rate * time_step,
                0.0,
                0.0,
            ]
        ),
        field_vector([0, 7, 2, 3, 4, 5, 6, 2]),
        field_vector([1, 1, 2, 3, 4, 5, 1, 2]),
        field_vector([1.0, 1.0, 0.0, 0.0, 0.0, 0.0, 1.0, 0.0]),
        field_vector([0, 0, 2, 3, 4, 5, 6, 1]),
        field_vector([1.0, -1.0, 1.0, 1.0, 1.0, 1.0, 1.0, 1.0]),
    )


def gathered(value, source):
    return picked(value[None], source)[0]


def bordering(value, tables, sign):
    first, second, factor = tables[6:9]
    return gathered(value, first) - (sign * factor) * gathered(value, second)


def border_terms(value, tables, north):
    term = viscosity * gathered(value, tables[9])
    return tables[10] * term if north else term


def spin_of(row, rad, spin_factor):
    radius = jnp.full((FIELDS, LANES), rad * ROWS + row, jnp.int32).astype(jnp.float32)
    distance = 1.0 + radius / (ROWS * RAD)
    return spin_factor / (distance * jnp.sqrt(distance))


def evolve(v, north, south, up, down, tables, spin):
    from_radial, from_vertical, from_spin, radial_factor, vertical_factor = tables[:5]
    laplacian = (north + south) + (up + down) - 4.0 * v
    rates = (
        radial_factor * picked(north - south, from_radial)
        + vertical_factor * picked(up - down, from_vertical)
        + spin * picked(v, from_spin)
    )
    return v + viscosity * laplacian + rates


def carry(source, target, speed, count):
    shape = (PART * FIELDS, LANES)
    forward = jnp.maximum(speed, 0.0)
    backward = jnp.minimum(speed, 0.0)
    hops = count // LANES
    lanes = lax.rem(count, LANES)
    lane = lax.broadcasted_iota(jnp.int32, shape, 1)
    own_mask = lane >= LANES - lanes
    low_mask = lane >= LANES - 1 - lanes
    high_mask = lane >= LANES + 1 - lanes
    next_mask = lane + lanes == 0

    def body(k, nothing):
        here = source[lax.rem(k - hops + AZ, AZ)].reshape(shape)
        before = source[lax.rem(k - hops + 2 * AZ - 1, AZ)].reshape(shape)
        after = source[lax.rem(k - hops + AZ + 1, AZ)].reshape(shape)
        cells = jnp.where(own_mask, before, here)
        lower = pltpu.roll(jnp.where(low_mask, before, here), 1, 1)
        upper = jnp.where(next_mask, after, jnp.where(high_mask, before, here))
        upper = pltpu.roll(upper, LANES - 1, 1)
        moved = cells - forward * (cells - lower) - backward * (upper - cells)
        target[k] = pltpu.roll(moved, lanes, 1).reshape(PART, FIELDS, LANES)
        return nothing

    lax.fori_loop(0, AZ, body, 0, unroll=8)


def kernel(
    state_hbm, counts_hbm, speeds_hbm, out,
    state, counts, speeds, packed, wide, evolved, *scratch,
):
    received = scratch[0:4]
    carried = scratch[4:8]
    ready = scratch[8:12]
    cell_below = scratch[12:16]
    cell_above = scratch[16:20]
    row_south, row_north, border_last, border_next = scratch[20:24]
    (in_send, in_recv, out_send, out_recv, own, up_send, up_recv, down_send, down_recv,
     row_send, row_recv, edge_send, edge_recv, load) = scratch[24:]

    loads = [
        pltpu.make_async_copy(source, target, load.at[i])
        for i, (source, target) in enumerate(
            [(state_hbm, state), (counts_hbm, counts), (speeds_hbm, speeds)]
        )
    ]

    me = lax.axis_index("az")
    rad = lax.axis_index("rad")
    rad_next = lax.rem(rad + 1, RAD)
    rad_last = lax.rem(rad + RAD - 1, RAD)
    block, quarter = place(me, rad)

    barrier = pltpu.get_barrier_semaphore()

    def greet(k, carry):
        pl.semaphore_signal(
            barrier, inc=1, device_id={"az": lax.rem(me + k, AZ)}, device_id_type=MESH
        )
        return carry

    lax.fori_loop(1, AZ, greet, 0)
    for other in (rad_next, rad_last):
        pl.semaphore_signal(barrier, inc=1, device_id={"rad": other}, device_id_type=MESH)

    for copy in loads:
        copy.start()
    tables = field_tables()
    for border in (row_south, row_north):
        border[pl.ds(BORDER, TILES), :] = jnp.zeros((TILES, LANES), jnp.float32)

    def pack(c):
        def body(i, carry):
            row = PART * i + c
            for cell in range(NZ):
                packed[row, cell] = state[pl.ds(cell * ROWS + row, FIELDS, stride=NZ * ROWS), :]
            return carry

        lax.fori_loop(0, ROWS // PART, body, 0)

    def partner(k):
        return lax.rem(me + AZ + (k + 1) // 2 * (2 * lax.rem(k, 2) - 1), AZ)

    def send_in(c):
        own_copy = pltpu.make_async_copy(
            packed.at[PART * block + c, pl.ds(PART * quarter, PART)], received[c].at[me], own.at[c]
        )
        own_copy.start()

        def body(k, carry):
            to = partner(k)
            to_block, to_quarter = place(to, rad)
            pltpu.make_async_remote_copy(
                src_ref=packed.at[PART * to_block + c, pl.ds(PART * to_quarter, PART)],
                dst_ref=received[c].at[me],
                send_sem=in_send.at[c],
                recv_sem=in_recv.at[c],
                device_id={"az": to},
                device_id_type=MESH,
            ).start()
            return carry

        lax.fori_loop(1, AZ, body, 0)
        return own_copy

    def send_out(c, part=0, cells=(0, 1, 2, 3)):
        first, count = cells[0], len(cells)
        target = wide.at[1 + PART * block + c, pl.ds(PART * quarter + first, count)]
        own_copy = pltpu.make_async_copy(
            ready[c].at[me, pl.ds(first, count)], target, own.at[PART + c if part == 0 else 2 * PART - 1 + part]
        )
        own_copy.start()
        which = c if part == 0 else PART - 1 + part

        def body(k, carry):
            to = partner(k)
            pltpu.make_async_remote_copy(
                src_ref=ready[c].at[to, pl.ds(first, count)],
                dst_ref=target,
                send_sem=out_send.at[which],
                recv_sem=out_recv.at[which],
                device_id={"az": to},
                device_id_type=MESH,
            ).start()
            return carry

        lax.fori_loop(1, AZ, body, 0)
        part_of = ready[c].at[pl.ds(0, AZ - 1), pl.ds(first, count)]
        return own_copy, pltpu.make_async_remote_copy(
            src_ref=part_of, dst_ref=part_of,
            send_sem=out_send.at[which], recv_sem=out_recv.at[which],
            device_id={"az": lax.rem(me + 1, AZ)}, device_id_type=MESH,
        )

    def whole(buffer, send_sem, recv_sem):
        part = buffer.at[pl.ds(0, AZ - 1)]
        return pltpu.make_async_remote_copy(
            src_ref=part, dst_ref=part, send_sem=send_sem, recv_sem=recv_sem,
            device_id={"az": lax.rem(me + 1, AZ)}, device_id_type=MESH,
        )

    def cells(c):
        to_down = owner(block, lax.rem(quarter + 3, 4), rad)
        to_up = owner(block, lax.rem(quarter + 1, 4), rad)
        down = pltpu.make_async_remote_copy(
            src_ref=carried[c].at[:, 0], dst_ref=cell_above[c],
            send_sem=down_send.at[c], recv_sem=down_recv.at[c],
            device_id={"az": to_down}, device_id_type=MESH,
        )
        up = pltpu.make_async_remote_copy(
            src_ref=carried[c].at[:, PART - 1], dst_ref=cell_below[c],
            send_sem=up_send.at[c], recv_sem=up_recv.at[c],
            device_id={"az": to_up}, device_id_type=MESH,
        )
        down.start()
        up.start()
        return down, up

    def row_copy(which, row, packing, target, sign):
        def body(k, nothing):
            value = row[k]
            for cell in range(PART):
                packing[pl.ds(k * PART + cell, FIELDS, stride=TILES), :] = bordering(
                    value[cell], tables, sign
                )
            return nothing

        lax.fori_loop(0, AZ, body, 0, unroll=2)
        step = -sign
        other = block + step
        to_rad = lax.rem(rad + (other + Z_CHIPS) // Z_CHIPS - 1 + RAD, RAD)
        to_block = lax.rem(other + Z_CHIPS, Z_CHIPS)
        copy = pltpu.make_async_remote_copy(
            src_ref=packing.at[pl.ds(0, BORDER)], dst_ref=target.at[pl.ds(0, BORDER)],
            send_sem=row_send.at[which], recv_sem=row_recv.at[which],
            device_id={"az": owner(to_block, quarter, to_rad), "rad": to_rad},
            device_id_type=MESH,
        )
        copy.start()
        return copy

    def first_step(c):
        row = PART * block + c
        carry(received[c], carried[c], speeds[row], counts[row])

    has_south = jnp.logical_or(rad > 0, block > 0)
    has_north = jnp.logical_or(rad < RAD - 1, block < Z_CHIPS - 1)

    def second_step(c):
        row = PART * block + c
        spin = spin_of(row, rad, tables[5])

        def body(k, nothing):
            v = carried[c][k]
            south = carried[c - 1][k] if c > 0 else jnp.zeros_like(v)
            north = carried[c + 1][k] if c < PART - 1 else jnp.zeros_like(v)
            up = jnp.concatenate([v[1:], cell_above[c][k][None]], axis=0)
            down = jnp.concatenate([cell_below[c][k][None], v[:-1]], axis=0)
            result = evolve(v, north, south, up, down, tables, spin)
            if c in (0, PART - 1):
                border, inside = (row_south, has_south) if c == 0 else (row_north, has_north)
                terms = jnp.stack(
                    [
                        border_terms(
                            border[pl.ds(k * PART + cell, FIELDS, stride=TILES), :], tables, c > 0
                        )
                        for cell in range(PART)
                    ]
                )
                result = result + jnp.where(inside, terms, jnp.zeros_like(terms))
            evolved[k] = result
            return nothing

        lax.fori_loop(0, AZ, body, 0, unroll=4)
        carry(evolved, ready[c], speeds[row], counts[row])

    ins, outs, halos = {}, {}, {}

    def wait_in(c):
        ins[c].wait()
        whole(received[c], in_send.at[c], in_recv.at[c]).wait_recv()

    def wait_cells(c):
        for copy in halos[c]:
            copy.wait_recv()

    def wait_out(c):
        outs[c][0].wait()
        outs[c][1].wait_recv()

    loads[0].wait()
    pack(0)
    pl.semaphore_wait(barrier, AZ + 1)
    ins[0] = send_in(0)
    pack(3)
    ins[3] = send_in(3)
    pack(1)
    pack(2)
    loads[1].wait()
    loads[2].wait()

    wait_in(0)
    ins[1] = send_in(1)
    first_step(0)
    to_last = row_copy(0, carried[0], border_last, row_north, 1)
    halos[0] = cells(0)

    wait_in(3)
    ins[2] = send_in(2)
    first_step(3)
    to_next = row_copy(1, carried[3], border_next, row_south, -1)
    halos[3] = cells(3)

    wait_in(1)
    first_step(1)
    halos[1] = cells(1)

    to_next.wait_recv()
    wait_cells(0)
    second_step(0)
    outs[0] = send_out(0)

    wait_in(2)
    first_step(2)
    halos[2] = cells(2)

    to_last.wait_recv()
    wait_cells(3)
    second_step(3)
    outs[3] = send_out(3)
    wait_cells(1)
    second_step(1)
    outs[1] = send_out(1)
    wait_cells(LAST)
    second_step(LAST)
    for part, cells_of_part in enumerate(LAST_PARTS):
        outs["last", part] = send_out(LAST, part, cells_of_part)

    def edge(which, source, target, to):
        copy = pltpu.make_async_remote_copy(
            src_ref=wide.at[source], dst_ref=wide.at[target],
            send_sem=edge_send.at[which], recv_sem=edge_recv.at[which],
            device_id={"rad": to}, device_id_type=MESH,
        )
        copy.start()
        return copy

    wait_out(0)
    edge_last = edge(0, 1, ROWS + 1, rad_last)
    wait_out(3)
    edge_next = edge(1, ROWS, 0, rad_next)
    edge_last.wait()
    edge_next.wait()

    @pl.when(rad == 0)
    def _():
        wide[0] = jnp.zeros((NZ, FIELDS, LANES), jnp.float32)

    @pl.when(rad == RAD - 1)
    def _():
        wide[ROWS + 1] = jnp.zeros((NZ, FIELDS, LANES), jnp.float32)

    def last(row, cells):
        spin = spin_of(row, rad, tables[5])
        for cell in cells:
            pick = lambda r, c: wide[r, c][None]
            result = evolve(
                pick(row + 1, cell), pick(row + 2, cell), pick(row, cell),
                pick(row + 1, (cell + 1) % NZ), pick(row + 1, (cell + NZ - 1) % NZ), tables, spin,
            )
            out[pl.ds(cell * ROWS + row, FIELDS, stride=NZ * ROWS), :] = result[0]

    def last_rows(work):
        def body(i, nothing):
            for c, cells in work:
                last(PART * i + c, [cell for cell in range(NZ) if cell % PART in cells])
            return nothing

        lax.fori_loop(0, ROWS // PART, body, 0)

    wait_out(1)
    last_rows([(0, range(PART))])
    arrived, done = set(), set()
    for part, cells_of_part in enumerate(LAST_PARTS):
        wait_out(("last", part))
        arrived |= set(cells_of_part)
        inner = {j for j in arrived if {(j + 1) % PART, (j + PART - 1) % PART} <= arrived}
        last_rows([(1, set(cells_of_part)), (3, set(cells_of_part)), (LAST, inner - done)])
        done |= inner

    for c in ORDER:
        whole(received[c], in_send.at[c], in_recv.at[c]).wait_send()
        for copy in halos[c]:
            copy.wait_send()
    for _, copy in outs.values():
        copy.wait_send()
    to_last.wait_send()
    to_next.wait_send()


def shards(state, shift_counts, residual_speed):
    circle = (AZ, PART, FIELDS, LANES)
    vmem = pl.BlockSpec(memory_space=pltpu.VMEM)
    hbm = pl.BlockSpec(memory_space=pltpu.HBM)
    f32 = jnp.float32
    dma = pltpu.SemaphoreType.DMA
    result = pl.pallas_call(
        kernel,
        out_shape=jax.ShapeDtypeStruct((FIELDS * NZ * ROWS, LANES), f32),
        in_specs=[hbm, hbm, hbm],
        out_specs=vmem,
        scratch_shapes=[
            pltpu.VMEM((FIELDS * NZ * ROWS, LANES), f32),
            pltpu.SMEM((ROWS,), jnp.int32),
            pltpu.SMEM((ROWS,), f32),
            pltpu.VMEM((ROWS, NZ, FIELDS, LANES), f32),
            pltpu.VMEM((ROWS + 2, NZ, FIELDS, LANES), f32),
            pltpu.VMEM(circle, f32),
        ]
        + [pltpu.VMEM(circle, f32)] * 12
        + [pltpu.VMEM((AZ, FIELDS, LANES), f32)] * 8
        + [pltpu.VMEM((FIELDS * TILES, LANES), f32)] * 4
        + [dma((4,)), dma((4,)), dma((8,)), dma((8,)), dma((12,))]
        + [dma((4,)), dma((4,)), dma((4,)), dma((4,))]
        + [dma((2,)), dma((2,)), dma((2,)), dma((2,)), dma((3,))],
        compiler_params=pltpu.CompilerParams(
            collective_id=0, has_side_effects=True, vmem_limit_bytes=50 << 20
        ),
    )(state.reshape(FIELDS * NZ * ROWS, LANES), shift_counts, residual_speed)
    return result.reshape(FIELDS, NZ, ROWS, LANES)


def solution(mesh):
    placed = (P(None, None, "rad", "az"), P("rad"), P("rad"))
    return jax.shard_map(
        shards, mesh=mesh, in_specs=placed, out_specs=P(None, None, "rad", "az"), check_vma=False
    )
```

```python
import jax
import jax.numpy as jnp
from jax import lax
from jax.experimental import pallas as pl
from jax.experimental.pallas import tpu as pltpu
from jax.sharding import PartitionSpec as P

FIELDS, NZ, ROWS, LANES = 8, 16, 32, 128
AZ, RAD = 32, 8
Z_CHIPS = 8
PART = 4
ORDER = (0, 3, 1, 2)
TILES = AZ * PART
BORDER = 7 * TILES
LAST = 2
LAST_PARTS = ((0, 1), (2,), (3,))

time_step = 0.2
viscosity = 0.1
shear_rate = 1.5

MESH = pl.DeviceIdType.MESH


def place(index, rad):
    core = lax.rem(index, 2)
    z = lax.rem(index // 2, Z_CHIPS)
    x = index // (2 * Z_CHIPS)
    block = z + lax.rem(rad, 2) * (Z_CHIPS - 1 - 2 * z)
    quarter = 2 * x + lax.rem(core + x, 2)
    return block, quarter


def owner(block, quarter, rad):
    z = block + lax.rem(rad, 2) * (Z_CHIPS - 1 - 2 * block)
    x = quarter // 2
    core = lax.rem(lax.rem(quarter, 2) + x, 2)
    return (x * Z_CHIPS + z) * 2 + core


def field_vector(values):
    row = lax.broadcasted_iota(jnp.int32, (FIELDS, LANES), 0)
    first = values[0]
    result = jnp.full((FIELDS, LANES), first, jnp.asarray(first).dtype)
    for index in range(1, FIELDS):
        result = jnp.where(row == index, values[index], result)
    return result


def picked(value, source):
    count = value.shape[0]
    flat = value.reshape(count * FIELDS, LANES)
    parts = [
        jnp.take_along_axis(flat[i * FIELDS : (i + 1) * FIELDS], source, axis=0)
        for i in range(count)
    ]
    return jnp.stack(parts)


def field_tables():
    half = 0.5 * time_step
    return (
        field_vector([1, 0, 2, 3, 4, 5, 1, 1]),
        field_vector([3, 4, 5, 0, 1, 2, 6, 3]),
        field_vector([0, 2, 1, 3, 4, 4, 6, 7]),
        field_vector([-half, -half, 0.0, 0.0, 0.0, 0.0, -half, -half]),
        field_vector([-half, half, half, -half, half, half, 0.0, -half]),
        field_vector(
            [
                0.0,
                2.0 * time_step,
                -(2.0 - shear_rate) * time_step,
                0.0,
                0.0,
                -shear_rate * time_step,
                0.0,
                0.0,
            ]
        ),
        field_vector([0, 7, 2, 3, 4, 5, 6, 2]),
        field_vector([1, 1, 2, 3, 4, 5, 1, 2]),
        field_vector([1.0, 1.0, 0.0, 0.0, 0.0, 0.0, 1.0, 0.0]),
        field_vector([0, 0, 2, 3, 4, 5, 6, 1]),
        field_vector([1.0, -1.0, 1.0, 1.0, 1.0, 1.0, 1.0, 1.0]),
    )


def gathered(value, source):
    return picked(value[None], source)[0]


def bordering(value, tables, sign):
    first, second, factor = tables[6:9]
    return gathered(value, first) - (sign * factor) * gathered(value, second)


def border_terms(value, tables, north):
    term = viscosity * gathered(value, tables[9])
    return tables[10] * term if north else term


def spin_of(row, rad, spin_factor):
    radius = jnp.full((FIELDS, LANES), rad * ROWS + row, jnp.int32).astype(jnp.float32)
    distance = 1.0 + radius / (ROWS * RAD)
    return spin_factor / (distance * jnp.sqrt(distance))


def evolve(v, north, south, up, down, tables, spin):
    from_radial, from_vertical, from_spin, radial_factor, vertical_factor = tables[:5]
    laplacian = (north + south) + (up + down) - 4.0 * v
    rates = (
        radial_factor * picked(north - south, from_radial)
        + vertical_factor * picked(up - down, from_vertical)
        + spin * picked(v, from_spin)
    )
    return v + viscosity * laplacian + rates


def carry(source, target, speed, count):
    shape = (PART * FIELDS, LANES)
    forward = jnp.maximum(speed, 0.0)
    backward = jnp.minimum(speed, 0.0)
    hops = count // LANES
    lanes = lax.rem(count, LANES)
    lane = lax.broadcasted_iota(jnp.int32, shape, 1)
    own_mask = lane >= LANES - lanes
    low_mask = lane >= LANES - 1 - lanes
    high_mask = lane >= LANES + 1 - lanes
    next_mask = lane + lanes == 0

    def body(k, nothing):
        here = source[lax.rem(k - hops + AZ, AZ)].reshape(shape)
        before = source[lax.rem(k - hops + 2 * AZ - 1, AZ)].reshape(shape)
        after = source[lax.rem(k - hops + AZ + 1, AZ)].reshape(shape)
        cells = jnp.where(own_mask, before, here)
        lower = pltpu.roll(jnp.where(low_mask, before, here), 1, 1)
        upper = jnp.where(next_mask, after, jnp.where(high_mask, before, here))
        upper = pltpu.roll(upper, LANES - 1, 1)
        moved = cells - forward * (cells - lower) - backward * (upper - cells)
        target[k] = pltpu.roll(moved, lanes, 1).reshape(PART, FIELDS, LANES)
        return nothing

    lax.fori_loop(0, AZ, body, 0, unroll=8)


def kernel(
    state_hbm, counts_hbm, speeds_hbm, out,
    state, counts, speeds, packed, wide, evolved, *scratch,
):
    received = scratch[0:4]
    carried = scratch[4:8]
    ready = scratch[8:12]
    cell_below = scratch[12:16]
    cell_above = scratch[16:20]
    row_south, row_north, border_last, border_next = scratch[20:24]
    (in_send, in_recv, out_send, out_recv, own, up_send, up_recv, down_send, down_recv,
     row_send, row_recv, edge_send, edge_recv, load) = scratch[24:]

    loads = [
        pltpu.make_async_copy(source, target, load.at[i])
        for i, (source, target) in enumerate(
            [(state_hbm, state), (counts_hbm, counts), (speeds_hbm, speeds)]
        )
    ]

    me = lax.axis_index("az")
    rad = lax.axis_index("rad")
    rad_next = lax.rem(rad + 1, RAD)
    rad_last = lax.rem(rad + RAD - 1, RAD)
    block, quarter = place(me, rad)

    for copy in loads:
        copy.start()
    barrier = pltpu.get_barrier_semaphore()

    def greet(k, carry):
        pl.semaphore_signal(
            barrier, inc=1, device_id={"az": lax.rem(me + k, AZ)}, device_id_type=MESH
        )
        return carry

    lax.fori_loop(1, AZ, greet, 0)
    for other in (rad_next, rad_last):
        pl.semaphore_signal(barrier, inc=1, device_id={"rad": other}, device_id_type=MESH)

    tables = field_tables()
    for border in (row_south, row_north):
        border[pl.ds(BORDER, TILES), :] = jnp.zeros((TILES, LANES), jnp.float32)

    def pack(c):
        def body(i, carry):
            row = PART * i + c
            for cell in range(NZ):
                packed[row, cell] = state[pl.ds(cell * ROWS + row, FIELDS, stride=NZ * ROWS), :]
            return carry

        lax.fori_loop(0, ROWS // PART, body, 0)

    def partner(k):
        return lax.rem(me + AZ + (k + 1) // 2 * (2 * lax.rem(k, 2) - 1), AZ)

    def send_in(c):
        own_copy = pltpu.make_async_copy(
            packed.at[PART * block + c, pl.ds(PART * quarter, PART)], received[c].at[me], own.at[c]
        )
        own_copy.start()

        def body(k, carry):
            to = partner(k)
            to_block, to_quarter = place(to, rad)
            pltpu.make_async_remote_copy(
                src_ref=packed.at[PART * to_block + c, pl.ds(PART * to_quarter, PART)],
                dst_ref=received[c].at[me],
                send_sem=in_send.at[c],
                recv_sem=in_recv.at[c],
                device_id={"az": to},
                device_id_type=MESH,
            ).start()
            return carry

        lax.fori_loop(1, AZ, body, 0)
        return own_copy

    def send_out(c, part=0, cells=(0, 1, 2, 3)):
        first, count = cells[0], len(cells)
        target = wide.at[1 + PART * block + c, pl.ds(PART * quarter + first, count)]
        own_copy = pltpu.make_async_copy(
            ready[c].at[me, pl.ds(first, count)], target, own.at[PART + c if part == 0 else 2 * PART - 1 + part]
        )
        own_copy.start()
        which = c if part == 0 else PART - 1 + part

        def body(k, carry):
            to = partner(k)
            pltpu.make_async_remote_copy(
                src_ref=ready[c].at[to, pl.ds(first, count)],
                dst_ref=target,
                send_sem=out_send.at[which],
                recv_sem=out_recv.at[which],
                device_id={"az": to},
                device_id_type=MESH,
            ).start()
            return carry

        lax.fori_loop(1, AZ, body, 0)
        part_of = ready[c].at[pl.ds(0, AZ - 1), pl.ds(first, count)]
        return own_copy, pltpu.make_async_remote_copy(
            src_ref=part_of, dst_ref=part_of,
            send_sem=out_send.at[which], recv_sem=out_recv.at[which],
            device_id={"az": lax.rem(me + 1, AZ)}, device_id_type=MESH,
        )

    def whole(buffer, send_sem, recv_sem):
        part = buffer.at[pl.ds(0, AZ - 1)]
        return pltpu.make_async_remote_copy(
            src_ref=part, dst_ref=part, send_sem=send_sem, recv_sem=recv_sem,
            device_id={"az": lax.rem(me + 1, AZ)}, device_id_type=MESH,
        )

    def cells(c):
        to_down = owner(block, lax.rem(quarter + 3, 4), rad)
        to_up = owner(block, lax.rem(quarter + 1, 4), rad)
        down = pltpu.make_async_remote_copy(
            src_ref=carried[c].at[:, 0], dst_ref=cell_above[c],
            send_sem=down_send.at[c], recv_sem=down_recv.at[c],
            device_id={"az": to_down}, device_id_type=MESH,
        )
        up = pltpu.make_async_remote_copy(
            src_ref=carried[c].at[:, PART - 1], dst_ref=cell_below[c],
            send_sem=up_send.at[c], recv_sem=up_recv.at[c],
            device_id={"az": to_up}, device_id_type=MESH,
        )
        down.start()
        up.start()
        return down, up

    def row_copy(which, row, packing, target, sign):
        def body(k, nothing):
            value = row[k]
            for cell in range(PART):
                packing[pl.ds(k * PART + cell, FIELDS, stride=TILES), :] = bordering(
                    value[cell], tables, sign
                )
            return nothing

        lax.fori_loop(0, AZ, body, 0, unroll=2)
        step = -sign
        other = block + step
        to_rad = lax.rem(rad + (other + Z_CHIPS) // Z_CHIPS - 1 + RAD, RAD)
        to_block = lax.rem(other + Z_CHIPS, Z_CHIPS)
        copy = pltpu.make_async_remote_copy(
            src_ref=packing.at[pl.ds(0, BORDER)], dst_ref=target.at[pl.ds(0, BORDER)],
            send_sem=row_send.at[which], recv_sem=row_recv.at[which],
            device_id={"az": owner(to_block, quarter, to_rad), "rad": to_rad},
            device_id_type=MESH,
        )
        copy.start()
        return copy

    def first_step(c):
        row = PART * block + c
        carry(received[c], carried[c], speeds[row], counts[row])

    has_south = jnp.logical_or(rad > 0, block > 0)
    has_north = jnp.logical_or(rad < RAD - 1, block < Z_CHIPS - 1)

    def second_step(c):
        row = PART * block + c
        spin = spin_of(row, rad, tables[5])

        def body(k, nothing):
            v = carried[c][k]
            south = carried[c - 1][k] if c > 0 else jnp.zeros_like(v)
            north = carried[c + 1][k] if c < PART - 1 else jnp.zeros_like(v)
            up = jnp.concatenate([v[1:], cell_above[c][k][None]], axis=0)
            down = jnp.concatenate([cell_below[c][k][None], v[:-1]], axis=0)
            result = evolve(v, north, south, up, down, tables, spin)
            if c in (0, PART - 1):
                border, inside = (row_south, has_south) if c == 0 else (row_north, has_north)
                terms = jnp.stack(
                    [
                        border_terms(
                            border[pl.ds(k * PART + cell, FIELDS, stride=TILES), :], tables, c > 0
                        )
                        for cell in range(PART)
                    ]
                )
                result = result + jnp.where(inside, terms, jnp.zeros_like(terms))
            evolved[k] = result
            return nothing

        lax.fori_loop(0, AZ, body, 0, unroll=4)
        carry(evolved, ready[c], speeds[row], counts[row])

    ins, outs, halos = {}, {}, {}

    def wait_in(c):
        ins[c].wait()
        whole(received[c], in_send.at[c], in_recv.at[c]).wait_recv()

    def wait_cells(c):
        for copy in halos[c]:
            copy.wait_recv()

    def wait_out(c):
        outs[c][0].wait()
        outs[c][1].wait_recv()

    loads[0].wait()
    pack(0)
    pl.semaphore_wait(barrier, AZ + 1)
    ins[0] = send_in(0)
    pack(3)
    ins[3] = send_in(3)
    pack(1)
    pack(2)
    loads[1].wait()
    loads[2].wait()

    wait_in(0)
    ins[1] = send_in(1)
    first_step(0)
    to_last = row_copy(0, carried[0], border_last, row_north, 1)
    halos[0] = cells(0)

    wait_in(3)
    first_step(3)
    to_next = row_copy(1, carried[3], border_next, row_south, -1)
    halos[3] = cells(3)

    wait_in(1)
    ins[2] = send_in(2)
    first_step(1)
    halos[1] = cells(1)

    to_next.wait_recv()
    wait_cells(0)
    second_step(0)
    outs[0] = send_out(0)

    wait_in(2)
    first_step(2)
    halos[2] = cells(2)

    to_last.wait_recv()
    wait_cells(3)
    second_step(3)
    outs[3] = send_out(3)
    wait_cells(1)
    second_step(1)
    outs[1] = send_out(1)
    wait_cells(LAST)
    second_step(LAST)
    for part, cells_of_part in enumerate(LAST_PARTS):
        outs["last", part] = send_out(LAST, part, cells_of_part)

    def edge(which, source, target, to):
        copy = pltpu.make_async_remote_copy(
            src_ref=wide.at[source], dst_ref=wide.at[target],
            send_sem=edge_send.at[which], recv_sem=edge_recv.at[which],
            device_id={"rad": to}, device_id_type=MESH,
        )
        copy.start()
        return copy

    wait_out(0)
    edge_last = edge(0, 1, ROWS + 1, rad_last)
    wait_out(3)
    edge_next = edge(1, ROWS, 0, rad_next)
    edge_last.wait()
    edge_next.wait()

    @pl.when(rad == 0)
    def _():
        wide[0] = jnp.zeros((NZ, FIELDS, LANES), jnp.float32)

    @pl.when(rad == RAD - 1)
    def _():
        wide[ROWS + 1] = jnp.zeros((NZ, FIELDS, LANES), jnp.float32)

    def last(row, cells):
        spin = spin_of(row, rad, tables[5])
        for cell in cells:
            pick = lambda r, c: wide[r, c][None]
            result = evolve(
                pick(row + 1, cell), pick(row + 2, cell), pick(row, cell),
                pick(row + 1, (cell + 1) % NZ), pick(row + 1, (cell + NZ - 1) % NZ), tables, spin,
            )
            out[pl.ds(cell * ROWS + row, FIELDS, stride=NZ * ROWS), :] = result[0]

    def last_rows(work):
        def body(i, nothing):
            for c, cells in work:
                last(PART * i + c, [cell for cell in range(NZ) if cell % PART in cells])
            return nothing

        lax.fori_loop(0, ROWS // PART, body, 0)

    wait_out(1)
    last_rows([(0, range(PART))])
    arrived, done = set(), set()
    for part, cells_of_part in enumerate(LAST_PARTS):
        wait_out(("last", part))
        arrived |= set(cells_of_part)
        inner = {j for j in arrived if {(j + 1) % PART, (j + PART - 1) % PART} <= arrived}
        last_rows([(1, set(cells_of_part)), (3, set(cells_of_part)), (LAST, inner - done)])
        done |= inner

    for c in ORDER:
        whole(received[c], in_send.at[c], in_recv.at[c]).wait_send()
        for copy in halos[c]:
            copy.wait_send()
    for _, copy in outs.values():
        copy.wait_send()
    to_last.wait_send()
    to_next.wait_send()


def shards(state, shift_counts, residual_speed):
    circle = (AZ, PART, FIELDS, LANES)
    vmem = pl.BlockSpec(memory_space=pltpu.VMEM)
    hbm = pl.BlockSpec(memory_space=pltpu.HBM)
    f32 = jnp.float32
    dma = pltpu.SemaphoreType.DMA
    result = pl.pallas_call(
        kernel,
        out_shape=jax.ShapeDtypeStruct((FIELDS * NZ * ROWS, LANES), f32),
        in_specs=[hbm, hbm, hbm],
        out_specs=vmem,
        scratch_shapes=[
            pltpu.VMEM((FIELDS * NZ * ROWS, LANES), f32),
            pltpu.SMEM((ROWS,), jnp.int32),
            pltpu.SMEM((ROWS,), f32),
            pltpu.VMEM((ROWS, NZ, FIELDS, LANES), f32),
            pltpu.VMEM((ROWS + 2, NZ, FIELDS, LANES), f32),
            pltpu.VMEM(circle, f32),
        ]
        + [pltpu.VMEM(circle, f32)] * 12
        + [pltpu.VMEM((AZ, FIELDS, LANES), f32)] * 8
        + [pltpu.VMEM((FIELDS * TILES, LANES), f32)] * 4
        + [dma((4,)), dma((4,)), dma((8,)), dma((8,)), dma((12,))]
        + [dma((4,)), dma((4,)), dma((4,)), dma((4,))]
        + [dma((2,)), dma((2,)), dma((2,)), dma((2,)), dma((3,))],
        compiler_params=pltpu.CompilerParams(
            collective_id=0, has_side_effects=True, vmem_limit_bytes=50 << 20
        ),
    )(state.reshape(FIELDS * NZ * ROWS, LANES), shift_counts, residual_speed)
    return result.reshape(FIELDS, NZ, ROWS, LANES)


def solution(mesh):
    placed = (P(None, None, "rad", "az"), P("rad"), P("rad"))
    return jax.shard_map(
        shards, mesh=mesh, in_specs=placed, out_specs=P(None, None, "rad", "az"), check_vma=False
    )
```

```python
import jax
import jax.numpy as jnp
from jax import lax
from jax.experimental import pallas as pl
from jax.experimental.pallas import tpu as pltpu
from jax.sharding import PartitionSpec as P

FIELDS, NZ, ROWS, LANES = 8, 16, 32, 128
AZ, RAD = 32, 8
Z_CHIPS = 8
PART = 4
ORDER = (0, 3, 1, 2)
TILES = AZ * PART
BORDER = 7 * TILES
LAST = 2
LAST_PARTS = ((0, 1), (2,), (3,))

time_step = 0.2
viscosity = 0.1
shear_rate = 1.5

MESH = pl.DeviceIdType.MESH


def place(index, rad):
    core = lax.rem(index, 2)
    z = lax.rem(index // 2, Z_CHIPS)
    x = index // (2 * Z_CHIPS)
    block = z + lax.rem(rad, 2) * (Z_CHIPS - 1 - 2 * z)
    quarter = 2 * x + lax.rem(core + x, 2)
    return block, quarter


def owner(block, quarter, rad):
    z = block + lax.rem(rad, 2) * (Z_CHIPS - 1 - 2 * block)
    x = quarter // 2
    core = lax.rem(lax.rem(quarter, 2) + x, 2)
    return (x * Z_CHIPS + z) * 2 + core


def field_vector(values):
    row = lax.broadcasted_iota(jnp.int32, (FIELDS, LANES), 0)
    first = values[0]
    result = jnp.full((FIELDS, LANES), first, jnp.asarray(first).dtype)
    for index in range(1, FIELDS):
        result = jnp.where(row == index, values[index], result)
    return result


def picked(value, source):
    count = value.shape[0]
    flat = value.reshape(count * FIELDS, LANES)
    parts = [
        jnp.take_along_axis(flat[i * FIELDS : (i + 1) * FIELDS], source, axis=0)
        for i in range(count)
    ]
    return jnp.stack(parts)


def field_tables():
    half = 0.5 * time_step
    return (
        field_vector([1, 0, 2, 3, 4, 5, 1, 1]),
        field_vector([3, 4, 5, 0, 1, 2, 6, 3]),
        field_vector([0, 2, 1, 3, 4, 4, 6, 7]),
        field_vector([-half, -half, 0.0, 0.0, 0.0, 0.0, -half, -half]),
        field_vector([-half, half, half, -half, half, half, 0.0, -half]),
        field_vector(
            [
                0.0,
                2.0 * time_step,
                -(2.0 - shear_rate) * time_step,
                0.0,
                0.0,
                -shear_rate * time_step,
                0.0,
                0.0,
            ]
        ),
        field_vector([0, 7, 2, 3, 4, 5, 6, 2]),
        field_vector([1, 1, 2, 3, 4, 5, 1, 2]),
        field_vector([1.0, 1.0, 0.0, 0.0, 0.0, 0.0, 1.0, 0.0]),
        field_vector([0, 0, 2, 3, 4, 5, 6, 1]),
        field_vector([1.0, -1.0, 1.0, 1.0, 1.0, 1.0, 1.0, 1.0]),
    )


def gathered(value, source):
    return picked(value[None], source)[0]


def bordering(value, tables, sign):
    first, second, factor = tables[6:9]
    return gathered(value, first) - (sign * factor) * gathered(value, second)


def border_terms(value, tables, north):
    term = viscosity * gathered(value, tables[9])
    return tables[10] * term if north else term


def spin_of(row, rad, spin_factor):
    radius = jnp.full((FIELDS, LANES), rad * ROWS + row, jnp.int32).astype(jnp.float32)
    distance = 1.0 + radius / (ROWS * RAD)
    return spin_factor / (distance * jnp.sqrt(distance))


def evolve(v, north, south, up, down, tables, spin):
    from_radial, from_vertical, from_spin, radial_factor, vertical_factor = tables[:5]
    laplacian = (north + south) + (up + down) - 4.0 * v
    rates = (
        radial_factor * picked(north - south, from_radial)
        + vertical_factor * picked(up - down, from_vertical)
        + spin * picked(v, from_spin)
    )
    return v + viscosity * laplacian + rates


def carry(source, target, speed, count):
    shape = (PART * FIELDS, LANES)
    forward = jnp.maximum(speed, 0.0)
    backward = jnp.minimum(speed, 0.0)
    hops = count // LANES
    lanes = lax.rem(count, LANES)
    lane = lax.broadcasted_iota(jnp.int32, shape, 1)
    own_mask = lane >= LANES - lanes
    low_mask = lane >= LANES - 1 - lanes
    high_mask = lane >= LANES + 1 - lanes
    next_mask = lane + lanes == 0

    def body(k, nothing):
        here = source[lax.rem(k - hops + AZ, AZ)].reshape(shape)
        before = source[lax.rem(k - hops + 2 * AZ - 1, AZ)].reshape(shape)
        after = source[lax.rem(k - hops + AZ + 1, AZ)].reshape(shape)
        cells = jnp.where(own_mask, before, here)
        lower = pltpu.roll(jnp.where(low_mask, before, here), 1, 1)
        upper = jnp.where(next_mask, after, jnp.where(high_mask, before, here))
        upper = pltpu.roll(upper, LANES - 1, 1)
        moved = cells - forward * (cells - lower) - backward * (upper - cells)
        target[k] = pltpu.roll(moved, lanes, 1).reshape(PART, FIELDS, LANES)
        return nothing

    lax.fori_loop(0, AZ, body, 0, unroll=8)


def kernel(
    state_hbm, counts_hbm, speeds_hbm, out,
    state, counts, speeds, packed, wide, evolved, *scratch,
):
    received = scratch[0:4]
    carried = scratch[4:8]
    ready = scratch[8:12]
    cell_below = scratch[12:16]
    cell_above = scratch[16:20]
    row_south, row_north, border_last, border_next = scratch[20:24]
    (in_send, in_recv, out_send, out_recv, own, up_send, up_recv, down_send, down_recv,
     row_send, row_recv, edge_send, edge_recv, load) = scratch[24:]

    loads = [
        pltpu.make_async_copy(source, target, load.at[i])
        for i, (source, target) in enumerate(
            [(state_hbm, state), (counts_hbm, counts), (speeds_hbm, speeds)]
        )
    ]

    me = lax.axis_index("az")
    rad = lax.axis_index("rad")
    rad_next = lax.rem(rad + 1, RAD)
    rad_last = lax.rem(rad + RAD - 1, RAD)
    block, quarter = place(me, rad)

    for copy in loads:
        copy.start()
    barrier = pltpu.get_barrier_semaphore()

    def greet(k, carry):
        pl.semaphore_signal(
            barrier, inc=1, device_id={"az": lax.rem(me + k, AZ)}, device_id_type=MESH
        )
        return carry

    lax.fori_loop(1, AZ, greet, 0)
    for other in (rad_next, rad_last):
        pl.semaphore_signal(barrier, inc=1, device_id={"rad": other}, device_id_type=MESH)

    tables = field_tables()
    for border in (row_south, row_north):
        border[pl.ds(BORDER, TILES), :] = jnp.zeros((TILES, LANES), jnp.float32)

    def pack(c):
        def body(i, carry):
            row = PART * i + c
            for cell in range(NZ):
                packed[row, cell] = state[pl.ds(cell * ROWS + row, FIELDS, stride=NZ * ROWS), :]
            return carry

        lax.fori_loop(0, ROWS // PART, body, 0)

    def partner(k):
        return lax.rem(me + AZ + (k + 1) // 2 * (2 * lax.rem(k, 2) - 1), AZ)

    def send_in(c):
        own_copy = pltpu.make_async_copy(
            packed.at[PART * block + c, pl.ds(PART * quarter, PART)], received[c].at[me], own.at[c]
        )
        own_copy.start()

        def body(k, carry):
            to = partner(k)
            to_block, to_quarter = place(to, rad)
            pltpu.make_async_remote_copy(
                src_ref=packed.at[PART * to_block + c, pl.ds(PART * to_quarter, PART)],
                dst_ref=received[c].at[me],
                send_sem=in_send.at[c],
                recv_sem=in_recv.at[c],
                device_id={"az": to},
                device_id_type=MESH,
            ).start()
            return carry

        lax.fori_loop(1, AZ, body, 0)
        return own_copy

    def send_out(c, slot, cells=(0, 1, 2, 3)):
        first, count = cells[0], len(cells)
        target = wide.at[1 + PART * block + c, pl.ds(PART * quarter + first, count)]
        own_copy = pltpu.make_async_copy(
            ready[c].at[me, pl.ds(first, count)], target, own.at[PART + slot]
        )
        own_copy.start()

        def body(k, carry):
            to = partner(k)
            pltpu.make_async_remote_copy(
                src_ref=ready[c].at[to, pl.ds(first, count)],
                dst_ref=target,
                send_sem=out_send.at[slot],
                recv_sem=out_recv.at[slot],
                device_id={"az": to},
                device_id_type=MESH,
            ).start()
            return carry

        lax.fori_loop(1, AZ, body, 0)
        part_of = ready[c].at[pl.ds(0, AZ - 1), pl.ds(first, count)]
        return own_copy, pltpu.make_async_remote_copy(
            src_ref=part_of, dst_ref=part_of,
            send_sem=out_send.at[slot], recv_sem=out_recv.at[slot],
            device_id={"az": lax.rem(me + 1, AZ)}, device_id_type=MESH,
        )

    def whole(buffer, send_sem, recv_sem):
        part = buffer.at[pl.ds(0, AZ - 1)]
        return pltpu.make_async_remote_copy(
            src_ref=part, dst_ref=part, send_sem=send_sem, recv_sem=recv_sem,
            device_id={"az": lax.rem(me + 1, AZ)}, device_id_type=MESH,
        )

    def cells(c):
        to_down = owner(block, lax.rem(quarter + 3, 4), rad)
        to_up = owner(block, lax.rem(quarter + 1, 4), rad)
        down = pltpu.make_async_remote_copy(
            src_ref=carried[c].at[:, 0], dst_ref=cell_above[c],
            send_sem=down_send.at[c], recv_sem=down_recv.at[c],
            device_id={"az": to_down}, device_id_type=MESH,
        )
        up = pltpu.make_async_remote_copy(
            src_ref=carried[c].at[:, PART - 1], dst_ref=cell_below[c],
            send_sem=up_send.at[c], recv_sem=up_recv.at[c],
            device_id={"az": to_up}, device_id_type=MESH,
        )
        down.start()
        up.start()
        return down, up

    def row_copy(which, row, packing, target, sign):
        def body(k, nothing):
            value = row[k]
            for cell in range(PART):
                packing[pl.ds(k * PART + cell, FIELDS, stride=TILES), :] = bordering(
                    value[cell], tables, sign
                )
            return nothing

        lax.fori_loop(0, AZ, body, 0, unroll=2)
        step = -sign
        other = block + step
        to_rad = lax.rem(rad + (other + Z_CHIPS) // Z_CHIPS - 1 + RAD, RAD)
        to_block = lax.rem(other + Z_CHIPS, Z_CHIPS)
        copy = pltpu.make_async_remote_copy(
            src_ref=packing.at[pl.ds(0, BORDER)], dst_ref=target.at[pl.ds(0, BORDER)],
            send_sem=row_send.at[which], recv_sem=row_recv.at[which],
            device_id={"az": owner(to_block, quarter, to_rad), "rad": to_rad},
            device_id_type=MESH,
        )
        copy.start()
        return copy

    def first_step(c):
        row = PART * block + c
        carry(received[c], carried[c], speeds[row], counts[row])

    has_south = jnp.logical_or(rad > 0, block > 0)
    has_north = jnp.logical_or(rad < RAD - 1, block < Z_CHIPS - 1)

    def second_step(c):
        row = PART * block + c
        spin = spin_of(row, rad, tables[5])

        def body(k, nothing):
            v = carried[c][k]
            south = carried[c - 1][k] if c > 0 else jnp.zeros_like(v)
            north = carried[c + 1][k] if c < PART - 1 else jnp.zeros_like(v)
            up = jnp.concatenate([v[1:], cell_above[c][k][None]], axis=0)
            down = jnp.concatenate([cell_below[c][k][None], v[:-1]], axis=0)
            result = evolve(v, north, south, up, down, tables, spin)
            if c in (0, PART - 1):
                border, inside = (row_south, has_south) if c == 0 else (row_north, has_north)
                terms = jnp.stack(
                    [
                        border_terms(
                            border[pl.ds(k * PART + cell, FIELDS, stride=TILES), :], tables, c > 0
                        )
                        for cell in range(PART)
                    ]
                )
                result = result + jnp.where(inside, terms, jnp.zeros_like(terms))
            evolved[k] = result
            return nothing

        lax.fori_loop(0, AZ, body, 0, unroll=4)
        carry(evolved, ready[c], speeds[row], counts[row])

    ins, outs, halos = {}, {}, {}

    def wait_in(c):
        ins[c].wait()
        whole(received[c], in_send.at[c], in_recv.at[c]).wait_recv()

    def wait_cells(c):
        for copy in halos[c]:
            copy.wait_recv()

    def wait_out(c):
        outs[c][0].wait()
        outs[c][1].wait_recv()

    loads[0].wait()
    pack(0)
    pl.semaphore_wait(barrier, AZ + 1)
    ins[0] = send_in(0)
    pack(3)
    pack(1)
    pack(2)
    ins[3] = send_in(3)
    loads[1].wait()
    loads[2].wait()

    wait_in(0)
    ins[1] = send_in(1)
    first_step(0)
    to_last = row_copy(0, carried[0], border_last, row_north, 1)
    halos[0] = cells(0)

    wait_in(3)
    first_step(3)
    to_next = row_copy(1, carried[3], border_next, row_south, -1)
    halos[3] = cells(3)

    wait_in(1)
    ins[2] = send_in(2)
    first_step(1)
    halos[1] = cells(1)

    to_next.wait_recv()
    wait_cells(0)
    second_step(0)
    outs[0] = send_out(0, 0, (0, 1))

    wait_in(2)
    outs["rest"] = send_out(0, LAST, (2, 3))
    first_step(2)
    halos[2] = cells(2)

    to_last.wait_recv()
    wait_cells(3)
    second_step(3)
    outs[3] = send_out(3, 3)
    wait_cells(1)
    second_step(1)
    outs[1] = send_out(1, 1)
    wait_cells(LAST)
    second_step(LAST)
    for part, cells_of_part in enumerate(LAST_PARTS):
        outs["last", part] = send_out(LAST, PART + part, cells_of_part)

    def edge(which, source, target, to):
        copy = pltpu.make_async_remote_copy(
            src_ref=wide.at[source], dst_ref=wide.at[target],
            send_sem=edge_send.at[which], recv_sem=edge_recv.at[which],
            device_id={"rad": to}, device_id_type=MESH,
        )
        copy.start()
        return copy

    wait_out(0)
    wait_out("rest")
    edge_last = edge(0, 1, ROWS + 1, rad_last)
    wait_out(3)
    edge_next = edge(1, ROWS, 0, rad_next)
    edge_last.wait()
    edge_next.wait()

    @pl.when(rad == 0)
    def _():
        wide[0] = jnp.zeros((NZ, FIELDS, LANES), jnp.float32)

    @pl.when(rad == RAD - 1)
    def _():
        wide[ROWS + 1] = jnp.zeros((NZ, FIELDS, LANES), jnp.float32)

    def last(row, cells):
        spin = spin_of(row, rad, tables[5])
        for cell in cells:
            pick = lambda r, c: wide[r, c][None]
            result = evolve(
                pick(row + 1, cell), pick(row + 2, cell), pick(row, cell),
                pick(row + 1, (cell + 1) % NZ), pick(row + 1, (cell + NZ - 1) % NZ), tables, spin,
            )
            out[pl.ds(cell * ROWS + row, FIELDS, stride=NZ * ROWS), :] = result[0]

    def last_rows(work):
        def body(i, nothing):
            for c, cells in work:
                last(PART * i + c, [cell for cell in range(NZ) if cell % PART in cells])
            return nothing

        lax.fori_loop(0, ROWS // PART, body, 0)

    wait_out(1)
    last_rows([(0, range(PART))])
    arrived, done = set(), set()
    for part, cells_of_part in enumerate(LAST_PARTS):
        wait_out(("last", part))
        arrived |= set(cells_of_part)
        inner = {j for j in arrived if {(j + 1) % PART, (j + PART - 1) % PART} <= arrived}
        last_rows([(1, set(cells_of_part)), (3, set(cells_of_part)), (LAST, inner - done)])
        done |= inner

    for c in ORDER:
        whole(received[c], in_send.at[c], in_recv.at[c]).wait_send()
        for copy in halos[c]:
            copy.wait_send()
    for _, copy in outs.values():
        copy.wait_send()
    to_last.wait_send()
    to_next.wait_send()


def shards(state, shift_counts, residual_speed):
    circle = (AZ, PART, FIELDS, LANES)
    vmem = pl.BlockSpec(memory_space=pltpu.VMEM)
    hbm = pl.BlockSpec(memory_space=pltpu.HBM)
    f32 = jnp.float32
    dma = pltpu.SemaphoreType.DMA
    result = pl.pallas_call(
        kernel,
        out_shape=jax.ShapeDtypeStruct((FIELDS * NZ * ROWS, LANES), f32),
        in_specs=[hbm, hbm, hbm],
        out_specs=vmem,
        scratch_shapes=[
            pltpu.VMEM((FIELDS * NZ * ROWS, LANES), f32),
            pltpu.SMEM((ROWS,), jnp.int32),
            pltpu.SMEM((ROWS,), f32),
            pltpu.VMEM((ROWS, NZ, FIELDS, LANES), f32),
            pltpu.VMEM((ROWS + 2, NZ, FIELDS, LANES), f32),
            pltpu.VMEM(circle, f32),
        ]
        + [pltpu.VMEM(circle, f32)] * 12
        + [pltpu.VMEM((AZ, FIELDS, LANES), f32)] * 8
        + [pltpu.VMEM((FIELDS * TILES, LANES), f32)] * 4
        + [dma((4,)), dma((4,)), dma((8,)), dma((8,)), dma((12,))]
        + [dma((4,)), dma((4,)), dma((4,)), dma((4,))]
        + [dma((2,)), dma((2,)), dma((2,)), dma((2,)), dma((3,))],
        compiler_params=pltpu.CompilerParams(
            collective_id=0, has_side_effects=True, vmem_limit_bytes=50 << 20
        ),
    )(state.reshape(FIELDS * NZ * ROWS, LANES), shift_counts, residual_speed)
    return result.reshape(FIELDS, NZ, ROWS, LANES)


def solution(mesh):
    placed = (P(None, None, "rad", "az"), P("rad"), P("rad"))
    return jax.shard_map(
        shards, mesh=mesh, in_specs=placed, out_specs=P(None, None, "rad", "az"), check_vma=False
    )
```

```python
import jax
import jax.numpy as jnp
from jax import lax
from jax.experimental import pallas as pl
from jax.experimental.pallas import tpu as pltpu
from jax.sharding import PartitionSpec as P

FIELDS, NZ, ROWS, LANES = 8, 16, 32, 128
AZ, RAD = 32, 8
Z_CHIPS = 8
PART = 4
ORDER = (0, 3, 1, 2)
TILES = AZ * PART
BORDER = 7 * TILES
LAST = 2
LAST_PARTS = ((0, 1, 2, 3),)

time_step = 0.2
viscosity = 0.1
shear_rate = 1.5

MESH = pl.DeviceIdType.MESH


def place(index, rad):
    core = lax.rem(index, 2)
    z = lax.rem(index // 2, Z_CHIPS)
    x = index // (2 * Z_CHIPS)
    block = z + lax.rem(rad, 2) * (Z_CHIPS - 1 - 2 * z)
    quarter = 2 * x + lax.rem(core + x, 2)
    return block, quarter


def owner(block, quarter, rad):
    z = block + lax.rem(rad, 2) * (Z_CHIPS - 1 - 2 * block)
    x = quarter // 2
    core = lax.rem(lax.rem(quarter, 2) + x, 2)
    return (x * Z_CHIPS + z) * 2 + core


def field_vector(values):
    row = lax.broadcasted_iota(jnp.int32, (FIELDS, LANES), 0)
    first = values[0]
    result = jnp.full((FIELDS, LANES), first, jnp.asarray(first).dtype)
    for index in range(1, FIELDS):
        result = jnp.where(row == index, values[index], result)
    return result


def picked(value, source):
    count = value.shape[0]
    flat = value.reshape(count * FIELDS, LANES)
    parts = [
        jnp.take_along_axis(flat[i * FIELDS : (i + 1) * FIELDS], source, axis=0)
        for i in range(count)
    ]
    return jnp.stack(parts)


def field_tables():
    half = 0.5 * time_step
    return (
        field_vector([1, 0, 2, 3, 4, 5, 1, 1]),
        field_vector([3, 4, 5, 0, 1, 2, 6, 3]),
        field_vector([0, 2, 1, 3, 4, 4, 6, 7]),
        field_vector([-half, -half, 0.0, 0.0, 0.0, 0.0, -half, -half]),
        field_vector([-half, half, half, -half, half, half, 0.0, -half]),
        field_vector(
            [
                0.0,
                2.0 * time_step,
                -(2.0 - shear_rate) * time_step,
                0.0,
                0.0,
                -shear_rate * time_step,
                0.0,
                0.0,
            ]
        ),
        field_vector([0, 7, 2, 3, 4, 5, 6, 2]),
        field_vector([1, 1, 2, 3, 4, 5, 1, 2]),
        field_vector([1.0, 1.0, 0.0, 0.0, 0.0, 0.0, 1.0, 0.0]),
        field_vector([0, 0, 2, 3, 4, 5, 6, 1]),
        field_vector([1.0, -1.0, 1.0, 1.0, 1.0, 1.0, 1.0, 1.0]),
    )


def gathered(value, source):
    return picked(value[None], source)[0]


def bordering(value, tables, sign):
    first, second, factor = tables[6:9]
    return gathered(value, first) - (sign * factor) * gathered(value, second)


def border_terms(value, tables, north):
    term = viscosity * gathered(value, tables[9])
    return tables[10] * term if north else term


def spin_of(row, rad, spin_factor):
    radius = jnp.full((FIELDS, LANES), rad * ROWS + row, jnp.int32).astype(jnp.float32)
    distance = 1.0 + radius / (ROWS * RAD)
    return spin_factor / (distance * jnp.sqrt(distance))


def evolve(v, north, south, up, down, tables, spin):
    from_radial, from_vertical, from_spin, radial_factor, vertical_factor = tables[:5]
    laplacian = (north + south) + (up + down) - 4.0 * v
    rates = (
        radial_factor * picked(north - south, from_radial)
        + vertical_factor * picked(up - down, from_vertical)
        + spin * picked(v, from_spin)
    )
    return v + viscosity * laplacian + rates


def carry(source, target, speed, count):
    shape = (PART * FIELDS, LANES)
    forward = jnp.maximum(speed, 0.0)
    backward = jnp.minimum(speed, 0.0)
    hops = count // LANES
    lanes = lax.rem(count, LANES)
    lane = lax.broadcasted_iota(jnp.int32, shape, 1)
    own_mask = lane >= LANES - lanes
    low_mask = lane >= LANES - 1 - lanes
    high_mask = lane >= LANES + 1 - lanes
    next_mask = lane + lanes == 0

    def body(k, nothing):
        here = source[lax.rem(k - hops + AZ, AZ)].reshape(shape)
        before = source[lax.rem(k - hops + 2 * AZ - 1, AZ)].reshape(shape)
        after = source[lax.rem(k - hops + AZ + 1, AZ)].reshape(shape)
        cells = jnp.where(own_mask, before, here)
        lower = pltpu.roll(jnp.where(low_mask, before, here), 1, 1)
        upper = jnp.where(next_mask, after, jnp.where(high_mask, before, here))
        upper = pltpu.roll(upper, LANES - 1, 1)
        moved = cells - forward * (cells - lower) - backward * (upper - cells)
        target[k] = pltpu.roll(moved, lanes, 1).reshape(PART, FIELDS, LANES)
        return nothing

    lax.fori_loop(0, AZ, body, 0, unroll=8)


def kernel(
    state_hbm, counts_hbm, speeds_hbm, out,
    state, counts, speeds, packed, wide, evolved, *scratch,
):
    received = scratch[0:4]
    carried = scratch[4:8]
    ready = scratch[8:12]
    cell_below = scratch[12:16]
    cell_above = scratch[16:20]
    row_south, row_north, border_last, border_next = scratch[20:24]
    (in_send, in_recv, out_send, out_recv, own, up_send, up_recv, down_send, down_recv,
     row_send, row_recv, edge_send, edge_recv, load) = scratch[24:]

    loads = [
        pltpu.make_async_copy(source, target, load.at[i])
        for i, (source, target) in enumerate(
            [(state_hbm, state), (counts_hbm, counts), (speeds_hbm, speeds)]
        )
    ]

    me = lax.axis_index("az")
    rad = lax.axis_index("rad")
    rad_next = lax.rem(rad + 1, RAD)
    rad_last = lax.rem(rad + RAD - 1, RAD)
    block, quarter = place(me, rad)

    for copy in loads:
        copy.start()
    barrier = pltpu.get_barrier_semaphore()

    def greet(k, carry):
        pl.semaphore_signal(
            barrier, inc=1, device_id={"az": lax.rem(me + k, AZ)}, device_id_type=MESH
        )
        return carry

    lax.fori_loop(1, AZ, greet, 0)
    for other in (rad_next, rad_last):
        pl.semaphore_signal(barrier, inc=1, device_id={"rad": other}, device_id_type=MESH)

    tables = field_tables()
    for border in (row_south, row_north):
        border[pl.ds(BORDER, TILES), :] = jnp.zeros((TILES, LANES), jnp.float32)

    def pack(c):
        def body(i, carry):
            row = PART * i + c
            for cell in range(NZ):
                packed[row, cell] = state[pl.ds(cell * ROWS + row, FIELDS, stride=NZ * ROWS), :]
            return carry

        lax.fori_loop(0, ROWS // PART, body, 0)

    def partner(k):
        return lax.rem(me + AZ + (k + 1) // 2 * (2 * lax.rem(k, 2) - 1), AZ)

    def send_in(c):
        own_copy = pltpu.make_async_copy(
            packed.at[PART * block + c, pl.ds(PART * quarter, PART)], received[c].at[me], own.at[c]
        )
        own_copy.start()

        def body(k, carry):
            to = partner(k)
            to_block, to_quarter = place(to, rad)
            pltpu.make_async_remote_copy(
                src_ref=packed.at[PART * to_block + c, pl.ds(PART * to_quarter, PART)],
                dst_ref=received[c].at[me],
                send_sem=in_send.at[c],
                recv_sem=in_recv.at[c],
                device_id={"az": to},
                device_id_type=MESH,
            ).start()
            return carry

        lax.fori_loop(1, AZ, body, 0)
        return own_copy

    def send_out(c, slot, cells=(0, 1, 2, 3)):
        first, count = cells[0], len(cells)
        target = wide.at[1 + PART * block + c, pl.ds(PART * quarter + first, count)]
        own_copy = pltpu.make_async_copy(
            ready[c].at[me, pl.ds(first, count)], target, own.at[PART + slot]
        )
        own_copy.start()

        def body(k, carry):
            to = partner(k)
            pltpu.make_async_remote_copy(
                src_ref=ready[c].at[to, pl.ds(first, count)],
                dst_ref=target,
                send_sem=out_send.at[slot],
                recv_sem=out_recv.at[slot],
                device_id={"az": to},
                device_id_type=MESH,
            ).start()
            return carry

        lax.fori_loop(1, AZ, body, 0)
        part_of = ready[c].at[pl.ds(0, AZ - 1), pl.ds(first, count)]
        return own_copy, pltpu.make_async_remote_copy(
            src_ref=part_of, dst_ref=part_of,
            send_sem=out_send.at[slot], recv_sem=out_recv.at[slot],
            device_id={"az": lax.rem(me + 1, AZ)}, device_id_type=MESH,
        )

    def whole(buffer, send_sem, recv_sem):
        part = buffer.at[pl.ds(0, AZ - 1)]
        return pltpu.make_async_remote_copy(
            src_ref=part, dst_ref=part, send_sem=send_sem, recv_sem=recv_sem,
            device_id={"az": lax.rem(me + 1, AZ)}, device_id_type=MESH,
        )

    def cells(c):
        to_down = owner(block, lax.rem(quarter + 3, 4), rad)
        to_up = owner(block, lax.rem(quarter + 1, 4), rad)
        down = pltpu.make_async_remote_copy(
            src_ref=carried[c].at[:, 0], dst_ref=cell_above[c],
            send_sem=down_send.at[c], recv_sem=down_recv.at[c],
            device_id={"az": to_down}, device_id_type=MESH,
        )
        up = pltpu.make_async_remote_copy(
            src_ref=carried[c].at[:, PART - 1], dst_ref=cell_below[c],
            send_sem=up_send.at[c], recv_sem=up_recv.at[c],
            device_id={"az": to_up}, device_id_type=MESH,
        )
        down.start()
        up.start()
        return down, up

    def row_copy(which, row, packing, target, sign):
        def body(k, nothing):
            value = row[k]
            for cell in range(PART):
                packing[pl.ds(k * PART + cell, FIELDS, stride=TILES), :] = bordering(
                    value[cell], tables, sign
                )
            return nothing

        lax.fori_loop(0, AZ, body, 0, unroll=2)
        step = -sign
        other = block + step
        to_rad = lax.rem(rad + (other + Z_CHIPS) // Z_CHIPS - 1 + RAD, RAD)
        to_block = lax.rem(other + Z_CHIPS, Z_CHIPS)
        copy = pltpu.make_async_remote_copy(
            src_ref=packing.at[pl.ds(0, BORDER)], dst_ref=target.at[pl.ds(0, BORDER)],
            send_sem=row_send.at[which], recv_sem=row_recv.at[which],
            device_id={"az": owner(to_block, quarter, to_rad), "rad": to_rad},
            device_id_type=MESH,
        )
        copy.start()
        return copy

    def first_step(c):
        row = PART * block + c
        carry(received[c], carried[c], speeds[row], counts[row])

    has_south = jnp.logical_or(rad > 0, block > 0)
    has_north = jnp.logical_or(rad < RAD - 1, block < Z_CHIPS - 1)

    def second_step(c):
        row = PART * block + c
        spin = spin_of(row, rad, tables[5])

        def body(k, nothing):
            v = carried[c][k]
            south = carried[c - 1][k] if c > 0 else jnp.zeros_like(v)
            north = carried[c + 1][k] if c < PART - 1 else jnp.zeros_like(v)
            up = jnp.concatenate([v[1:], cell_above[c][k][None]], axis=0)
            down = jnp.concatenate([cell_below[c][k][None], v[:-1]], axis=0)
            result = evolve(v, north, south, up, down, tables, spin)
            if c in (0, PART - 1):
                border, inside = (row_south, has_south) if c == 0 else (row_north, has_north)
                terms = jnp.stack(
                    [
                        border_terms(
                            border[pl.ds(k * PART + cell, FIELDS, stride=TILES), :], tables, c > 0
                        )
                        for cell in range(PART)
                    ]
                )
                result = result + jnp.where(inside, terms, jnp.zeros_like(terms))
            evolved[k] = result
            return nothing

        lax.fori_loop(0, AZ, body, 0, unroll=4)
        carry(evolved, ready[c], speeds[row], counts[row])

    ins, outs, halos = {}, {}, {}

    def wait_in(c):
        ins[c].wait()
        whole(received[c], in_send.at[c], in_recv.at[c]).wait_recv()

    def wait_cells(c):
        for copy in halos[c]:
            copy.wait_recv()

    def wait_out(c):
        outs[c][0].wait()
        outs[c][1].wait_recv()

    loads[0].wait()
    pack(0)
    pl.semaphore_wait(barrier, AZ + 1)
    ins[0] = send_in(0)
    pack(3)
    pack(1)
    pack(2)
    ins[3] = send_in(3)
    loads[1].wait()
    loads[2].wait()

    wait_in(0)
    ins[1] = send_in(1)
    first_step(0)
    to_last = row_copy(0, carried[0], border_last, row_north, 1)
    halos[0] = cells(0)

    wait_in(3)
    first_step(3)
    to_next = row_copy(1, carried[3], border_next, row_south, -1)
    halos[3] = cells(3)

    wait_in(1)
    ins[2] = send_in(2)
    first_step(1)
    halos[1] = cells(1)

    to_next.wait_recv()
    wait_cells(0)
    second_step(0)
    outs[0] = send_out(0, 0, (0, 1))

    wait_in(2)
    outs["rest"] = send_out(0, LAST, (2, 3))
    first_step(2)
    halos[2] = cells(2)

    to_last.wait_recv()
    wait_cells(3)
    second_step(3)
    outs[3] = send_out(3, 3)
    wait_cells(1)
    second_step(1)
    outs[1] = send_out(1, 1)
    wait_cells(LAST)
    second_step(LAST)
    for part, cells_of_part in enumerate(LAST_PARTS):
        outs["last", part] = send_out(LAST, PART + part, cells_of_part)

    def edge(which, source, target, to):
        copy = pltpu.make_async_remote_copy(
            src_ref=wide.at[source], dst_ref=wide.at[target],
            send_sem=edge_send.at[which], recv_sem=edge_recv.at[which],
            device_id={"rad": to}, device_id_type=MESH,
        )
        copy.start()
        return copy

    wait_out(0)
    wait_out("rest")
    edge_last = edge(0, 1, ROWS + 1, rad_last)
    wait_out(3)
    edge_next = edge(1, ROWS, 0, rad_next)
    edge_last.wait()
    edge_next.wait()

    @pl.when(rad == 0)
    def _():
        wide[0] = jnp.zeros((NZ, FIELDS, LANES), jnp.float32)

    @pl.when(rad == RAD - 1)
    def _():
        wide[ROWS + 1] = jnp.zeros((NZ, FIELDS, LANES), jnp.float32)

    def last(row, cells):
        spin = spin_of(row, rad, tables[5])
        for cell in cells:
            pick = lambda r, c: wide[r, c][None]
            result = evolve(
                pick(row + 1, cell), pick(row + 2, cell), pick(row, cell),
                pick(row + 1, (cell + 1) % NZ), pick(row + 1, (cell + NZ - 1) % NZ), tables, spin,
            )
            out[pl.ds(cell * ROWS + row, FIELDS, stride=NZ * ROWS), :] = result[0]

    def last_rows(work):
        def body(i, nothing):
            for c, cells in work:
                last(PART * i + c, [cell for cell in range(NZ) if cell % PART in cells])
            return nothing

        lax.fori_loop(0, ROWS // PART, body, 0)

    wait_out(1)
    last_rows([(0, range(PART))])
    arrived, done = set(), set()
    for part, cells_of_part in enumerate(LAST_PARTS):
        wait_out(("last", part))
        arrived |= set(cells_of_part)
        inner = {j for j in arrived if {(j + 1) % PART, (j + PART - 1) % PART} <= arrived}
        last_rows([(1, set(cells_of_part)), (3, set(cells_of_part)), (LAST, inner - done)])
        done |= inner

    for c in ORDER:
        whole(received[c], in_send.at[c], in_recv.at[c]).wait_send()
        for copy in halos[c]:
            copy.wait_send()
    for _, copy in outs.values():
        copy.wait_send()
    to_last.wait_send()
    to_next.wait_send()


def shards(state, shift_counts, residual_speed):
    circle = (AZ, PART, FIELDS, LANES)
    vmem = pl.BlockSpec(memory_space=pltpu.VMEM)
    hbm = pl.BlockSpec(memory_space=pltpu.HBM)
    f32 = jnp.float32
    dma = pltpu.SemaphoreType.DMA
    result = pl.pallas_call(
        kernel,
        out_shape=jax.ShapeDtypeStruct((FIELDS * NZ * ROWS, LANES), f32),
        in_specs=[hbm, hbm, hbm],
        out_specs=vmem,
        scratch_shapes=[
            pltpu.VMEM((FIELDS * NZ * ROWS, LANES), f32),
            pltpu.SMEM((ROWS,), jnp.int32),
            pltpu.SMEM((ROWS,), f32),
            pltpu.VMEM((ROWS, NZ, FIELDS, LANES), f32),
            pltpu.VMEM((ROWS + 2, NZ, FIELDS, LANES), f32),
            pltpu.VMEM(circle, f32),
        ]
        + [pltpu.VMEM(circle, f32)] * 12
        + [pltpu.VMEM((AZ, FIELDS, LANES), f32)] * 8
        + [pltpu.VMEM((FIELDS * TILES, LANES), f32)] * 4
        + [dma((4,)), dma((4,)), dma((8,)), dma((8,)), dma((12,))]
        + [dma((4,)), dma((4,)), dma((4,)), dma((4,))]
        + [dma((2,)), dma((2,)), dma((2,)), dma((2,)), dma((3,))],
        compiler_params=pltpu.CompilerParams(
            collective_id=0, has_side_effects=True, vmem_limit_bytes=50 << 20
        ),
    )(state.reshape(FIELDS * NZ * ROWS, LANES), shift_counts, residual_speed)
    return result.reshape(FIELDS, NZ, ROWS, LANES)


def solution(mesh):
    placed = (P(None, None, "rad", "az"), P("rad"), P("rad"))
    return jax.shard_map(
        shards, mesh=mesh, in_specs=placed, out_specs=P(None, None, "rad", "az"), check_vma=False
    )
```

```python
import jax
import jax.numpy as jnp
from jax import lax
from jax.experimental import pallas as pl
from jax.experimental.pallas import tpu as pltpu
from jax.sharding import PartitionSpec as P

FIELDS, NZ, ROWS, LANES = 8, 16, 32, 128
AZ, RAD = 32, 8
Z_CHIPS = 8
PART = 4
ORDER = (0, 3, 1, 2)
TILES = AZ * PART
BORDER = 7 * TILES
LAST = 2
LAST_PARTS = ((0, 1, 2, 3),)

time_step = 0.2
viscosity = 0.1
shear_rate = 1.5

MESH = pl.DeviceIdType.MESH


def place(index, rad):
    core = lax.rem(index, 2)
    z = lax.rem(index // 2, Z_CHIPS)
    x = index // (2 * Z_CHIPS)
    block = z + lax.rem(rad, 2) * (Z_CHIPS - 1 - 2 * z)
    quarter = 2 * x + lax.rem(core + x, 2)
    return block, quarter


def owner(block, quarter, rad):
    z = block + lax.rem(rad, 2) * (Z_CHIPS - 1 - 2 * block)
    x = quarter // 2
    core = lax.rem(lax.rem(quarter, 2) + x, 2)
    return (x * Z_CHIPS + z) * 2 + core


def field_vector(values):
    row = lax.broadcasted_iota(jnp.int32, (FIELDS, LANES), 0)
    first = values[0]
    result = jnp.full((FIELDS, LANES), first, jnp.asarray(first).dtype)
    for index in range(1, FIELDS):
        result = jnp.where(row == index, values[index], result)
    return result


def picked(value, source):
    count = value.shape[0]
    flat = value.reshape(count * FIELDS, LANES)
    parts = [
        jnp.take_along_axis(flat[i * FIELDS : (i + 1) * FIELDS], source, axis=0)
        for i in range(count)
    ]
    return jnp.stack(parts)


def field_tables():
    half = 0.5 * time_step
    return (
        field_vector([1, 0, 2, 3, 4, 5, 1, 1]),
        field_vector([3, 4, 5, 0, 1, 2, 6, 3]),
        field_vector([0, 2, 1, 3, 4, 4, 6, 7]),
        field_vector([-half, -half, 0.0, 0.0, 0.0, 0.0, -half, -half]),
        field_vector([-half, half, half, -half, half, half, 0.0, -half]),
        field_vector(
            [
                0.0,
                2.0 * time_step,
                -(2.0 - shear_rate) * time_step,
                0.0,
                0.0,
                -shear_rate * time_step,
                0.0,
                0.0,
            ]
        ),
        field_vector([0, 7, 2, 3, 4, 5, 6, 2]),
        field_vector([1, 1, 2, 3, 4, 5, 1, 2]),
        field_vector([1.0, 1.0, 0.0, 0.0, 0.0, 0.0, 1.0, 0.0]),
        field_vector([0, 0, 2, 3, 4, 5, 6, 1]),
        field_vector([1.0, -1.0, 1.0, 1.0, 1.0, 1.0, 1.0, 1.0]),
    )


def gathered(value, source):
    return picked(value[None], source)[0]


def bordering(value, tables, sign):
    first, second, factor = tables[6:9]
    return gathered(value, first) - (sign * factor) * gathered(value, second)


def border_terms(value, tables, north):
    term = viscosity * gathered(value, tables[9])
    return tables[10] * term if north else term


def spin_of(row, rad, spin_factor):
    radius = jnp.full((FIELDS, LANES), rad * ROWS + row, jnp.int32).astype(jnp.float32)
    distance = 1.0 + radius / (ROWS * RAD)
    return spin_factor / (distance * jnp.sqrt(distance))


def evolve(v, north, south, up, down, tables, spin):
    from_radial, from_vertical, from_spin, radial_factor, vertical_factor = tables[:5]
    laplacian = (north + south) + (up + down) - 4.0 * v
    rates = (
        radial_factor * picked(north - south, from_radial)
        + vertical_factor * picked(up - down, from_vertical)
        + spin * picked(v, from_spin)
    )
    return v + viscosity * laplacian + rates


def carry(source, target, speed, count):
    shape = (PART * FIELDS, LANES)
    forward = jnp.maximum(speed, 0.0)
    backward = jnp.minimum(speed, 0.0)
    hops = count // LANES
    lanes = lax.rem(count, LANES)
    lane = lax.broadcasted_iota(jnp.int32, shape, 1)
    own_mask = lane >= LANES - lanes
    low_mask = lane >= LANES - 1 - lanes
    high_mask = lane >= LANES + 1 - lanes
    next_mask = lane + lanes == 0

    def body(k, nothing):
        here = source[lax.rem(k - hops + AZ, AZ)].reshape(shape)
        before = source[lax.rem(k - hops + 2 * AZ - 1, AZ)].reshape(shape)
        after = source[lax.rem(k - hops + AZ + 1, AZ)].reshape(shape)
        cells = jnp.where(own_mask, before, here)
        lower = pltpu.roll(jnp.where(low_mask, before, here), 1, 1)
        upper = jnp.where(next_mask, after, jnp.where(high_mask, before, here))
        upper = pltpu.roll(upper, LANES - 1, 1)
        moved = cells - forward * (cells - lower) - backward * (upper - cells)
        target[k] = pltpu.roll(moved, lanes, 1).reshape(PART, FIELDS, LANES)
        return nothing

    lax.fori_loop(0, AZ, body, 0, unroll=8)


def kernel(
    state_hbm, counts_hbm, speeds_hbm, out,
    state, counts, speeds, packed, wide, evolved, *scratch,
):
    received = scratch[0:4]
    carried = scratch[4:8]
    ready = scratch[8:12]
    cell_below = scratch[12:16]
    cell_above = scratch[16:20]
    row_south, row_north, border_last, border_next = scratch[20:24]
    (in_send, in_recv, out_send, out_recv, own, up_send, up_recv, down_send, down_recv,
     row_send, row_recv, edge_send, edge_recv, load) = scratch[24:]

    loads = [
        pltpu.make_async_copy(source, target, load.at[i])
        for i, (source, target) in enumerate(
            [(state_hbm, state), (counts_hbm, counts), (speeds_hbm, speeds)]
        )
    ]

    me = lax.axis_index("az")
    rad = lax.axis_index("rad")
    rad_next = lax.rem(rad + 1, RAD)
    rad_last = lax.rem(rad + RAD - 1, RAD)
    block, quarter = place(me, rad)

    for copy in loads:
        copy.start()
    barrier = pltpu.get_barrier_semaphore()

    for other in (rad_next, rad_last):
        pl.semaphore_signal(barrier, inc=1, device_id={"rad": other}, device_id_type=MESH)

    def greet(k, carry):
        pl.semaphore_signal(
            barrier, inc=1, device_id={"az": lax.rem(me + k, AZ)}, device_id_type=MESH
        )
        return carry

    lax.fori_loop(1, AZ, greet, 0)

    tables = field_tables()
    for border in (row_south, row_north):
        border[pl.ds(BORDER, TILES), :] = jnp.zeros((TILES, LANES), jnp.float32)

    def pack(c):
        def body(i, carry):
            row = PART * i + c
            for cell in range(NZ):
                packed[row, cell] = state[pl.ds(cell * ROWS + row, FIELDS, stride=NZ * ROWS), :]
            return carry

        lax.fori_loop(0, ROWS // PART, body, 0)

    def partner(k):
        return lax.rem(me + AZ + (k + 1) // 2 * (2 * lax.rem(k, 2) - 1), AZ)

    def send_in(c):
        own_copy = pltpu.make_async_copy(
            packed.at[PART * block + c, pl.ds(PART * quarter, PART)], received[c].at[me], own.at[c]
        )
        own_copy.start()

        def body(k, carry):
            to = partner(k)
            to_block, to_quarter = place(to, rad)
            pltpu.make_async_remote_copy(
                src_ref=packed.at[PART * to_block + c, pl.ds(PART * to_quarter, PART)],
                dst_ref=received[c].at[me],
                send_sem=in_send.at[c],
                recv_sem=in_recv.at[c],
                device_id={"az": to},
                device_id_type=MESH,
            ).start()
            return carry

        lax.fori_loop(1, AZ, body, 0)
        return own_copy

    def send_out(c, slot, cells=(0, 1, 2, 3)):
        first, count = cells[0], len(cells)
        target = wide.at[1 + PART * block + c, pl.ds(PART * quarter + first, count)]
        own_copy = pltpu.make_async_copy(
            ready[c].at[me, pl.ds(first, count)], target, own.at[PART + slot]
        )
        own_copy.start()

        def body(k, carry):
            to = partner(k)
            pltpu.make_async_remote_copy(
                src_ref=ready[c].at[to, pl.ds(first, count)],
                dst_ref=target,
                send_sem=out_send.at[slot],
                recv_sem=out_recv.at[slot],
                device_id={"az": to},
                device_id_type=MESH,
            ).start()
            return carry

        lax.fori_loop(1, AZ, body, 0)
        part_of = ready[c].at[pl.ds(0, AZ - 1), pl.ds(first, count)]
        return own_copy, pltpu.make_async_remote_copy(
            src_ref=part_of, dst_ref=part_of,
            send_sem=out_send.at[slot], recv_sem=out_recv.at[slot],
            device_id={"az": lax.rem(me + 1, AZ)}, device_id_type=MESH,
        )

    def whole(buffer, send_sem, recv_sem):
        part = buffer.at[pl.ds(0, AZ - 1)]
        return pltpu.make_async_remote_copy(
            src_ref=part, dst_ref=part, send_sem=send_sem, recv_sem=recv_sem,
            device_id={"az": lax.rem(me + 1, AZ)}, device_id_type=MESH,
        )

    def cells(c):
        to_down = owner(block, lax.rem(quarter + 3, 4), rad)
        to_up = owner(block, lax.rem(quarter + 1, 4), rad)
        down = pltpu.make_async_remote_copy(
            src_ref=carried[c].at[:, 0], dst_ref=cell_above[c],
            send_sem=down_send.at[c], recv_sem=down_recv.at[c],
            device_id={"az": to_down}, device_id_type=MESH,
        )
        up = pltpu.make_async_remote_copy(
            src_ref=carried[c].at[:, PART - 1], dst_ref=cell_below[c],
            send_sem=up_send.at[c], recv_sem=up_recv.at[c],
            device_id={"az": to_up}, device_id_type=MESH,
        )
        down.start()
        up.start()
        return down, up

    def row_copy(which, row, packing, target, sign):
        def body(k, nothing):
            value = row[k]
            for cell in range(PART):
                packing[pl.ds(k * PART + cell, FIELDS, stride=TILES), :] = bordering(
                    value[cell], tables, sign
                )
            return nothing

        lax.fori_loop(0, AZ, body, 0, unroll=2)
        step = -sign
        other = block + step
        to_rad = lax.rem(rad + (other + Z_CHIPS) // Z_CHIPS - 1 + RAD, RAD)
        to_block = lax.rem(other + Z_CHIPS, Z_CHIPS)
        copy = pltpu.make_async_remote_copy(
            src_ref=packing.at[pl.ds(0, BORDER)], dst_ref=target.at[pl.ds(0, BORDER)],
            send_sem=row_send.at[which], recv_sem=row_recv.at[which],
            device_id={"az": owner(to_block, quarter, to_rad), "rad": to_rad},
            device_id_type=MESH,
        )
        copy.start()
        return copy

    def first_step(c):
        row = PART * block + c
        carry(received[c], carried[c], speeds[row], counts[row])

    has_south = jnp.logical_or(rad > 0, block > 0)
    has_north = jnp.logical_or(rad < RAD - 1, block < Z_CHIPS - 1)

    def second_step(c):
        row = PART * block + c
        spin = spin_of(row, rad, tables[5])

        def body(k, nothing):
            v = carried[c][k]
            south = carried[c - 1][k] if c > 0 else jnp.zeros_like(v)
            north = carried[c + 1][k] if c < PART - 1 else jnp.zeros_like(v)
            up = jnp.concatenate([v[1:], cell_above[c][k][None]], axis=0)
            down = jnp.concatenate([cell_below[c][k][None], v[:-1]], axis=0)
            result = evolve(v, north, south, up, down, tables, spin)
            if c in (0, PART - 1):
                border, inside = (row_south, has_south) if c == 0 else (row_north, has_north)
                terms = jnp.stack(
                    [
                        border_terms(
                            border[pl.ds(k * PART + cell, FIELDS, stride=TILES), :], tables, c > 0
                        )
                        for cell in range(PART)
                    ]
                )
                result = result + jnp.where(inside, terms, jnp.zeros_like(terms))
            evolved[k] = result
            return nothing

        lax.fori_loop(0, AZ, body, 0, unroll=4)
        carry(evolved, ready[c], speeds[row], counts[row])

    ins, outs, halos = {}, {}, {}

    def wait_in(c):
        ins[c].wait()
        whole(received[c], in_send.at[c], in_recv.at[c]).wait_recv()

    def wait_cells(c):
        for copy in halos[c]:
            copy.wait_recv()

    def wait_out(c):
        outs[c][0].wait()
        outs[c][1].wait_recv()

    loads[0].wait()
    pack(0)
    pl.semaphore_wait(barrier, AZ + 1)
    ins[0] = send_in(0)
    pack(3)
    pack(1)
    pack(2)
    ins[3] = send_in(3)
    loads[1].wait()
    loads[2].wait()

    wait_in(0)
    ins[1] = send_in(1)
    first_step(0)
    halos[0] = cells(0)
    to_last = row_copy(0, carried[0], border_last, row_north, 1)

    wait_in(3)
    first_step(3)
    to_next = row_copy(1, carried[3], border_next, row_south, -1)
    halos[3] = cells(3)

    wait_in(1)
    ins[2] = send_in(2)
    first_step(1)

    to_next.wait_recv()
    wait_cells(0)
    second_step(0)
    outs[0] = send_out(0, 0, (0, 1))

    halos[1] = cells(1)
    wait_in(2)
    outs["rest"] = send_out(0, LAST, (2, 3))
    first_step(2)
    halos[2] = cells(2)

    to_last.wait_recv()
    wait_cells(3)
    second_step(3)
    outs[3] = send_out(3, 3)
    wait_cells(1)
    second_step(1)
    outs[1] = send_out(1, 1)
    wait_cells(LAST)
    second_step(LAST)
    for part, cells_of_part in enumerate(LAST_PARTS):
        outs["last", part] = send_out(LAST, PART + part, cells_of_part)

    def edge(which, source, target, to):
        copy = pltpu.make_async_remote_copy(
            src_ref=wide.at[source], dst_ref=wide.at[target],
            send_sem=edge_send.at[which], recv_sem=edge_recv.at[which],
            device_id={"rad": to}, device_id_type=MESH,
        )
        copy.start()
        return copy

    wait_out(0)
    wait_out("rest")
    edge_last = edge(0, 1, ROWS + 1, rad_last)
    wait_out(3)
    edge_next = edge(1, ROWS, 0, rad_next)
    edge_last.wait()
    edge_next.wait()

    @pl.when(rad == 0)
    def _():
        wide[0] = jnp.zeros((NZ, FIELDS, LANES), jnp.float32)

    @pl.when(rad == RAD - 1)
    def _():
        wide[ROWS + 1] = jnp.zeros((NZ, FIELDS, LANES), jnp.float32)

    def last(row, cells):
        spin = spin_of(row, rad, tables[5])
        for cell in cells:
            pick = lambda r, c: wide[r, c][None]
            result = evolve(
                pick(row + 1, cell), pick(row + 2, cell), pick(row, cell),
                pick(row + 1, (cell + 1) % NZ), pick(row + 1, (cell + NZ - 1) % NZ), tables, spin,
            )
            out[pl.ds(cell * ROWS + row, FIELDS, stride=NZ * ROWS), :] = result[0]

    def last_rows(work):
        def body(i, nothing):
            for c, cells in work:
                last(PART * i + c, [cell for cell in range(NZ) if cell % PART in cells])
            return nothing

        lax.fori_loop(0, ROWS // PART, body, 0)

    wait_out(1)
    last_rows([(0, range(PART))])
    arrived, done = set(), set()
    for part, cells_of_part in enumerate(LAST_PARTS):
        wait_out(("last", part))
        arrived |= set(cells_of_part)
        inner = {j for j in arrived if {(j + 1) % PART, (j + PART - 1) % PART} <= arrived}
        last_rows([(1, set(cells_of_part)), (3, set(cells_of_part)), (LAST, inner - done)])
        done |= inner

    for c in ORDER:
        whole(received[c], in_send.at[c], in_recv.at[c]).wait_send()
        for copy in halos[c]:
            copy.wait_send()
    for _, copy in outs.values():
        copy.wait_send()
    to_last.wait_send()
    to_next.wait_send()


def shards(state, shift_counts, residual_speed):
    circle = (AZ, PART, FIELDS, LANES)
    vmem = pl.BlockSpec(memory_space=pltpu.VMEM)
    hbm = pl.BlockSpec(memory_space=pltpu.HBM)
    f32 = jnp.float32
    dma = pltpu.SemaphoreType.DMA
    result = pl.pallas_call(
        kernel,
        out_shape=jax.ShapeDtypeStruct((FIELDS * NZ * ROWS, LANES), f32),
        in_specs=[hbm, hbm, hbm],
        out_specs=vmem,
        scratch_shapes=[
            pltpu.VMEM((FIELDS * NZ * ROWS, LANES), f32),
            pltpu.SMEM((ROWS,), jnp.int32),
            pltpu.SMEM((ROWS,), f32),
            pltpu.VMEM((ROWS, NZ, FIELDS, LANES), f32),
            pltpu.VMEM((ROWS + 2, NZ, FIELDS, LANES), f32),
            pltpu.VMEM(circle, f32),
        ]
        + [pltpu.VMEM(circle, f32)] * 12
        + [pltpu.VMEM((AZ, FIELDS, LANES), f32)] * 8
        + [pltpu.VMEM((FIELDS * TILES, LANES), f32)] * 4
        + [dma((4,)), dma((4,)), dma((8,)), dma((8,)), dma((12,))]
        + [dma((4,)), dma((4,)), dma((4,)), dma((4,))]
        + [dma((2,)), dma((2,)), dma((2,)), dma((2,)), dma((3,))],
        compiler_params=pltpu.CompilerParams(
            collective_id=0, has_side_effects=True, vmem_limit_bytes=50 << 20
        ),
    )(state.reshape(FIELDS * NZ * ROWS, LANES), shift_counts, residual_speed)
    return result.reshape(FIELDS, NZ, ROWS, LANES)


def solution(mesh):
    placed = (P(None, None, "rad", "az"), P("rad"), P("rad"))
    return jax.shard_map(
        shards, mesh=mesh, in_specs=placed, out_specs=P(None, None, "rad", "az"), check_vma=False
    )
```
